32 devices in a mesh: seq: 16 (over z, y, x), tp: 2 (over core).
Axes of the slice: x: 2, y: 2, z: 4, core: 2. Of those that a mesh axis runs over, the one named last changes fastest.
Arguments:
- teacher_rows: bfloat16 [7680, 8192], P('seq', 'tp'), may hold values from -2700 to 2700, as said below
- teacher_gain: float32 [8192], P('tp'), may hold values from 0.1 to 1.9
- teacher_counts: int32 [16], replicated, may hold values from 288 to 480, as said below
- projector: bfloat16 [8192, 4096], P('tp', 'seq'), may hold values from -0.0625 to 0.0625
- student_rows: bfloat16 [6144, 4096], P('seq', 'tp'), may hold values from -2700 to 2700
- student_gain: float32 [4096], P('tp'), may hold values from 0.1 to 1.9
- span_shift: int32 [48], P('seq'), may hold values from -128 to 128, as said below
- span_len: int32 [48], P('seq'), may hold values from 64 to 128
- align_weights: bfloat16 [6144, 128], P('seq'), may hold values from 0.0099487305 to 1
Outputs:
- row_grad: bfloat16 [6144, 4096], P('seq', 'tp')
- gain_grad: float32 [4096], P('tp')
The draws below stay inside these ranges and needn't reach their ends.
Inputs may be any that keep to these rules, and one draw needn't show every extreme that they name: `teacher_counts`: the counts of indices 2m and 2m + 1 add up to 768; one index holds exactly 480 rows in every draw. `teacher_rows`: slots at or beyond an index's count hold no part of the sequence. `span_shift`: for the first block of each index of seq (k = 0) the shift lies in -128 .. -64; for the last (k = 2) it is 128.
All inputs are finite; a program needn't handle non-finite values.
Results may differ from the reference program's by a relative error of at most 0.014.
Values may be sent and summed in bfloat16 or wider, within the bound.
A program may use at most 128 MiB of HBM per device.

```python
import math
import jax
import jax.numpy as jnp
from jax import lax

DT = 8192
DS = 4096
BLOCK = 128
BLK_DEV = 3
ROWS_DEV = 384
SPREAD = 96
JITTER = 128
TCAP = 480
SEQ_ROWS = 6144
BLOCKS = 48
N_SEQ = 16
N_TP = 2


def tilted_rows(key, row_count, width):
    keys = jax.random.split(key, 4)
    base_values = jnp.clip(jax.random.normal(keys[0], (row_count, width), jnp.float32), -6.0, 6.0)
    tilt = jax.random.uniform(keys[1], (row_count, 1), jnp.float32, 0.5, 1.5)
    column_place = jnp.arange(width, dtype=jnp.float32) / width
    roughness = jax.random.uniform(keys[2], (1, width), jnp.float32, 0.7, 1.4)
    row_scale = jnp.exp(jax.random.uniform(keys[3], (row_count, 1), jnp.float32, 0.0, 2.3))
    return base_values * jnp.exp(2.3 * tilt * column_place[None, :]) * roughness * row_scale


def draw_teacher_rows(key, part):
    return tilted_rows(jax.random.fold_in(key, 11), N_SEQ * TCAP, DT).astype(jnp.bfloat16)


def draw_student_rows(key, part):
    return tilted_rows(jax.random.fold_in(key, 23), ROWS_DEV * N_SEQ, DS).astype(jnp.bfloat16)


def draw_teacher_counts(key, part):
    keys = jax.random.split(jax.random.fold_in(key, 37), 2)
    half_count = N_SEQ // 2
    deviation = jax.random.randint(keys[0], (half_count,), 0 - SPREAD, SPREAD + 1)
    chosen = jax.random.randint(keys[1], (), 0, half_count)
    deviation = jnp.where(jnp.arange(half_count) == chosen, SPREAD, deviation)
    paired = jnp.stack([ROWS_DEV + deviation, ROWS_DEV - deviation], axis=1)
    return paired.reshape(N_SEQ).astype(jnp.int32)


def draw_span_shift(key, part):
    keys = jax.random.split(jax.random.fold_in(key, 53), 2)
    within = jnp.arange(BLK_DEV * N_SEQ, dtype=jnp.int32) % BLK_DEV
    general = jax.random.randint(keys[0], (BLK_DEV * N_SEQ,), 0 - JITTER, JITTER + 1)
    first = jax.random.randint(keys[1], (BLK_DEV * N_SEQ,), 0 - JITTER, 0 - JITTER // 2 + 1)
    last = jnp.full((BLK_DEV * N_SEQ,), JITTER, jnp.int32)
    shift = jnp.where(within == 0, first, jnp.where(within == BLK_DEV - 1, last, general))
    return shift.astype(jnp.int32)


def plant(array, own_key, least, largest):
    spot = [jax.random.randint(jax.random.fold_in(own_key, axis), (), 0, length) for axis, length in enumerate(array.shape)]
    longest = array.shape.index(max(array.shape))
    beside = spot[:longest] + [(spot[longest] + 1) % array.shape[longest]] + spot[longest + 1:]
    return array.at[tuple(spot)].set(least).at[tuple(beside)].set(largest)


def levels(key, extent, cuts, low, top_value):
    factor_of, own = 1.0, jax.random.fold_in(key, 6)
    for dim, parts in cuts:
        draws = jnp.exp(jax.random.uniform(jax.random.fold_in(own, dim), (parts,), jnp.float32, low / len(cuts), top_value / len(cuts)))
        factor_of = factor_of * jnp.repeat(draws, extent[dim] // parts).reshape([-1 if axis == dim else 1 for axis in range(len(extent))])
    return factor_of


def centred(stream_key, dims, scale, limit, cuts=(), kind=jnp.bfloat16):
    entries = jax.random.normal(stream_key, dims, jnp.float32) * scale
    if len(cuts) > 0:
        entries = levels(stream_key, dims, cuts, -0.22, 0.18) * entries
    return jnp.clip(entries, min=-limit, max=limit).astype(kind)


def setup_inputs(seed: int = 0) -> dict:
    seeds = jax.random.split(jax.random.key(seed), 10)
    teacher_rows = draw_teacher_rows(jax.random.fold_in(seeds[9], 71), 0)
    teacher_gain = jnp.clip(1.0 + 0.18 * jax.random.normal(seeds[1], (DT,), jnp.float32), 0.1, 1.9)
    teacher_counts = draw_teacher_counts(jax.random.fold_in(seeds[9], 71), 0)
    projector = centred(seeds[3], (DT, DS), DT ** -0.5, 0.0625, ((0, 2), (1, 16)))
    student_rows = draw_student_rows(jax.random.fold_in(seeds[9], 71), 0)
    student_gain = jnp.clip(1.0 + 0.18 * jax.random.normal(seeds[5], (DS,), jnp.float32), 0.1, 1.9)
    span_shift = draw_span_shift(jax.random.fold_in(seeds[9], 71), 0)
    span_len = plant(jax.random.randint(seeds[7], (BLOCKS,), BLOCK // 2, BLOCK + 1), jax.random.fold_in(seeds[7], 1), BLOCK // 2, BLOCK).astype(jnp.int32)
    align_weights = jnp.clip(jnp.exp(math.log(1.0) - 4.61031033 * jax.random.uniform(seeds[8], (SEQ_ROWS, BLOCK), jnp.float32) ** levels(seeds[8], (SEQ_ROWS, BLOCK), ((0, 16),), -0.2, 0.2)), 0.0099487305, 1.0).astype(jnp.bfloat16)
    return {"teacher_rows": teacher_rows, "teacher_gain": teacher_gain, "teacher_counts": teacher_counts, "projector": projector, "student_rows": student_rows, "student_gain": student_gain, "span_shift": span_shift, "span_len": span_len, "align_weights": align_weights}


epsilon = 1e-06

def reference(teacher_rows, teacher_gain, teacher_counts, projector, student_rows, student_gain, span_shift, span_len, align_weights):
    seq_rows = ROWS_DEV * N_SEQ
    starts = (jnp.cumsum(teacher_counts) - teacher_counts).astype(jnp.int32)
    positions = jnp.arange(seq_rows, dtype=jnp.int32)
    owner_device = (lax.optimization_barrier(jnp.sum((positions[:, None] >= starts[None, :]).astype(jnp.int32), axis=1)) - 1).astype(jnp.int32)
    source = (owner_device * TCAP + positions - jnp.take(starts, owner_device)).astype(jnp.int32)
    teacher_seq = jnp.take(teacher_rows, source, axis=0).astype(jnp.float32)
    teacher_scale = lax.rsqrt(lax.optimization_barrier(jnp.sum(teacher_seq * teacher_seq, axis=1)) / DT + epsilon)
    teacher_normed = (teacher_seq * teacher_scale[:, None] * teacher_gain.astype(jnp.float32)[None, :]).astype(jnp.bfloat16)
    group_width = DT // N_TP

    def add_group(group_index, accumulated):
        left_part = lax.dynamic_slice_in_dim(teacher_normed, group_index * group_width, group_width, 1)
        right_part = lax.dynamic_slice_in_dim(projector, group_index * group_width, group_width, 0)
        partial_sum = jnp.dot(left_part, right_part, preferred_element_type=jnp.float32).astype(jnp.bfloat16)
        partial_sum = lax.optimization_barrier(partial_sum)
        return accumulated + partial_sum.astype(jnp.float32)
    mapped = lax.fori_loop(0, N_TP, add_group, jnp.zeros((seq_rows, DS), jnp.float32)).astype(jnp.bfloat16)
    block_ids = jnp.arange(BLK_DEV * N_SEQ, dtype=jnp.int32)
    device = (block_ids // BLK_DEV).astype(jnp.int32)
    within = (block_ids % BLK_DEV).astype(jnp.int32)
    block_count = jnp.take(teacher_counts, device)
    span_start = jnp.take(starts, device) + within * block_count // BLK_DEV + span_shift
    span_start = jnp.clip(span_start, 0, seq_rows - span_len).astype(jnp.int32)
    offsets = jnp.arange(BLOCK, dtype=jnp.int32)
    window_index = jnp.clip(span_start[:, None] + offsets[None, :], 0, seq_rows - 1).astype(jnp.int32)
    live_mask = offsets[None, :] < span_len[:, None]
    weights = align_weights.reshape(BLK_DEV * N_SEQ, BLOCK, BLOCK)
    weights = jnp.where(live_mask[:, None, :], weights, jnp.zeros_like(weights))

    def mix_block(block_args):
        block_weights, block_index = block_args
        window = jnp.take(mapped, block_index, axis=0)
        return jnp.dot(block_weights, window, preferred_element_type=jnp.float32)
    target = lax.map(mix_block, (weights, window_index)).reshape(seq_rows, DS)
    target_hat = target * lax.rsqrt(lax.optimization_barrier(jnp.sum(target * target, axis=1, keepdims=True)) / DS + epsilon)
    student = student_rows.astype(jnp.float32)
    student_scale = lax.rsqrt(lax.optimization_barrier(jnp.sum(student * student, axis=1, keepdims=True)) / DS + epsilon)
    student_hat = student * student_scale
    residual = student_hat * student_gain[None, :] - target_hat
    weighted = residual * student_gain[None, :]
    inner_mean = lax.optimization_barrier(jnp.sum(weighted * student_hat, axis=1, keepdims=True)) / DS
    row_grad = (student_scale * (weighted - student_hat * inner_mean)).astype(jnp.bfloat16)
    gain_grad = lax.optimization_barrier(jnp.sum(residual * student_hat, axis=0)) / seq_rows
    return (row_grad, gain_grad)
```

```python
import functools

import jax
import jax.numpy as jnp
from jax import lax
from jax.experimental import pallas as pl
from jax.experimental.pallas import tpu as pltpu
from jax.sharding import PartitionSpec as P

epsilon = 1e-06
MESH = pl.DeviceIdType.MESH
VMEM_LIMIT = 52 * 1024 * 1024


def group_size(count):
    size = 1
    while size * size < count:
        size *= 2
    return size


def partner(p, e, g):
    if g == 4:
        if e == 0:
            return p, p
        low, high = 1 - 2 * (p % 2), 2 - 4 * (p // 2)
        other = p + (low if e % 2 else 0) + (high if e // 2 else 0)
        return other, other
    return (p - e + g) % g, (p + e) % g


def gather_kernel(
    g, nq, tp, nh,
    x_hbm, p_hbm, w_hbm, a_hbm,
    mapped, w_all, a_all,
    xs, ps, part, recv,
    x_send, x_recv, u_send, d_send, p_recv, s_send, s_recv, t_send, t_recv, local,
):
    me, t = lax.axis_index("seq"), lax.axis_index("tp")
    p, q = me % g, me // g
    base = q * g
    half = xs.shape[1]
    nl = nq // tp

    barrier = pltpu.get_barrier_semaphore()
    for e in range(1, g):
        pl.semaphore_signal(barrier, inc=1, device_id=(base + (p + e) % g, t), device_id_type=MESH)
    for o in range(1, tp):
        pl.semaphore_signal(barrier, inc=1, device_id=(me, (t + o) % tp), device_id_type=MESH)

    @pl.when(q > 0)
    def _():
        pl.semaphore_signal(barrier, inc=1, device_id=(me - g, t), device_id_type=MESH)

    @pl.when(q < nq - 1)
    def _():
        pl.semaphore_signal(barrier, inc=1, device_id=(me + g, t), device_id_type=MESH)

    ends = (q == 0).astype(jnp.int32) + (q == nq - 1).astype(jnp.int32)
    pl.semaphore_wait(barrier, g - 1 + tp - 1 + 2 - ends)

    def x_copy(source, e, h, member):
        return pltpu.make_async_remote_copy(
            src_ref=source, dst_ref=xs.at[e * nh + h],
            send_sem=x_send.at[e * nh + h], recv_sem=x_recv.at[e * nh + h],
            device_id=(base + member, t), device_id_type=MESH,
        )

    def own(h):
        return x_hbm.at[pl.ds(h * half, half)]

    def p_copy(source, block, sem, seq):
        return pltpu.make_async_remote_copy(
            src_ref=source, dst_ref=ps.at[block], send_sem=sem, recv_sem=p_recv.at[block],
            device_id=(seq, t), device_id_type=MESH,
        )

    relayed = g == 4
    direct = [1, 2] if relayed else list(range(1, g))

    def up(s):
        return p_copy(p_hbm if s == 0 else ps.at[q - s], q - s, u_send.at[s], me + g)

    def down(s):
        return p_copy(p_hbm if s == 0 else ps.at[q + s], q + s, d_send.at[s], me - g)

    def forward(s):
        @pl.when(q - s >= 0)
        def _():
            if s > 0:
                p_copy(p_hbm, q - s, u_send.at[0], me).wait_recv()

            @pl.when(q < nq - 1)
            def _():
                up(s).start()

        @pl.when(q + s < nq)
        def _():
            if s > 0:
                p_copy(p_hbm, q + s, u_send.at[0], me).wait_recv()

            @pl.when(q > 0)
            def _():
                down(s).start()

    first = []
    for h in range(nh):
        for e in direct:
            k = nh - 1 - h if e == 2 else h
            first.append((e, k))
    for e, h in first[: len(direct)]:
        x_copy(own(h), e, h, partner(p, e, g)[1]).start()
    forward(0)
    for e, h in first[len(direct):]:
        x_copy(own(h), e, h, partner(p, e, g)[1]).start()

    smalls = []
    for index, (source, target) in enumerate(((w_hbm, w_all), (a_hbm, a_all))):
        for e in range(1, g):
            copy = pltpu.make_async_remote_copy(
                src_ref=source, dst_ref=target.at[p],
                send_sem=s_send.at[index, e], recv_sem=s_recv.at[index, e],
                device_id=(base + (p + e) % g, t), device_id_type=MESH,
            )
            copy.start()
            smalls.append(copy)
    locals_ = [
        pltpu.make_async_copy(p_hbm, ps.at[q], local.at[0]),
        pltpu.make_async_copy(w_hbm, w_all.at[p], local.at[1]),
        pltpu.make_async_copy(a_hbm, a_all.at[p], local.at[2]),
    ]
    for h in range(nh):
        locals_.append(pltpu.make_async_copy(own(h), xs.at[h], local.at[3 + h]))
    for copy in locals_:
        copy.start()
    for copy in locals_:
        copy.wait()

    def multiply(c0, c1, b0, b1):
        def blocks(b, carry):
            def chunks(c, inner):
                part[b, c] = jnp.dot(
                    xs[c], ps[b], preferred_element_type=jnp.float32
                ).astype(jnp.bfloat16)
                return inner

            return lax.fori_loop(c0, c1, chunks, carry)

        lax.fori_loop(b0, b1, blocks, 0)

    def near(s):
        return jnp.maximum(q - s, 0), jnp.minimum(q + s, nq - 1) + 1

    def at_distance(s, c0, c1):
        @pl.when(q - s >= 0)
        def _():
            multiply(c0, c1, q - s, q - s + 1)

        @pl.when(q + s < nq)
        def _():
            multiply(c0, c1, q + s, q + s + 1)

    for e, h in first[: len(direct)]:
        copy = x_copy(own(h), e, h, partner(p, e, g)[1])
        copy.wait_recv()
        if relayed:
            x_copy(xs.at[e * nh + h], 3, h, partner(p, 3 - e, g)[1]).start()
    forward(1)
    for e, h in first[len(direct):]:
        x_copy(own(h), e, h, partner(p, e, g)[1]).wait_recv()
    early = (1 + len(direct)) * nh
    multiply(0, early, *near(1))
    for s in range(2, nq - 1):
        forward(s)
        at_distance(s, 0, early)
    if relayed:
        for h in range(nh):
            x_copy(xs.at[3 * nh + h], 3, h, p).wait_recv()
        multiply(early, g * nh, *near(nq - 2))
    forward(nq - 1)
    at_distance(nq - 1, 0, g * nh)

    sums = []
    for o in range(1, tp):
        other = (t + o) % tp
        copy = pltpu.make_async_remote_copy(
            src_ref=part.at[pl.ds(other * nl, nl)], dst_ref=recv.at[o - 1],
            send_sem=t_send.at[o - 1], recv_sem=t_recv.at[o - 1],
            device_id=(me, other), device_id_type=MESH,
        )
        copy.start()
        sums.append(copy)
    for copy in smalls + sums:
        copy.wait()

    def add(i, carry):
        block, chunk = i // (g * nh), i % (g * nh)
        total = part[t * nl + block, chunk].astype(jnp.float32)
        for o in range(1, tp):
            total += recv[o - 1, block, chunk].astype(jnp.float32)
        mapped[block, chunk] = total.astype(jnp.bfloat16)
        return carry

    lax.fori_loop(0, nl * g * nh, add, 0)

    for e, h in first:
        x_copy(own(h), e, h, partner(p, e, g)[1]).wait_send()
    if relayed:
        for e, h in first[: len(direct)]:
            x_copy(xs.at[e * nh + h], 3, h, partner(p, 3 - e, g)[1]).wait_send()
    for s in range(nq - 1):
        @pl.when((q - s >= 0) & (q < nq - 1))
        def _():
            up(s).wait_send()

        @pl.when((q + s < nq) & (q > 0))
        def _():
            down(s).wait_send()


def gather_map(g, nq, tp, x, p, w, a):
    rows, depth = x.shape
    width = p.shape[1]
    nh = 2 if rows % 32 == 0 else 1
    half = rows // nh
    nl = nq // tp
    any_spec = pl.BlockSpec(memory_space=pl.ANY)
    vmem = pl.BlockSpec(memory_space=pltpu.VMEM)
    dma = pltpu.SemaphoreType.DMA
    return pl.pallas_call(
        functools.partial(gather_kernel, g, nq, tp, nh),
        out_shape=(
            jax.ShapeDtypeStruct((nl, g * nh, half, width), jnp.bfloat16),
            jax.ShapeDtypeStruct((g,) + w.shape, w.dtype),
            jax.ShapeDtypeStruct((g,) + a.shape, a.dtype),
        ),
        in_specs=[any_spec] * 4,
        out_specs=(vmem, vmem, vmem),
        scratch_shapes=[
            pltpu.VMEM((g * nh, half, depth), jnp.bfloat16),
            pltpu.VMEM((nq, depth, width), jnp.bfloat16),
            pltpu.VMEM((nq, g * nh, half, width), jnp.bfloat16),
            pltpu.VMEM((max(tp - 1, 1), nl, g * nh, half, width), jnp.bfloat16),
            dma((g * nh,)),
            dma((g * nh,)),
            dma((nq,)),
            dma((nq,)),
            dma((nq,)),
            dma((2, g)),
            dma((2, g)),
            dma((tp,)),
            dma((tp,)),
            dma((3 + nh,)),
        ],
        compiler_params=pltpu.CompilerParams(
            collective_id=0, has_side_effects=True, vmem_limit_bytes=VMEM_LIMIT
        ),
        cost_estimate=pl.CostEstimate(
            flops=2 * g * rows * depth * nq * width,
            bytes_accessed=2 * (g * rows * depth + nq * depth * width),
            transcendentals=0,
        ),
    )(x, p, w, a)


def sum_kernel(n, value, total, held, send_sem, recv_sem):
    me, t = lax.axis_index("seq"), lax.axis_index("tp")
    barrier = pltpu.get_barrier_semaphore()
    for o in range(1, n):
        pl.semaphore_signal(barrier, inc=1, device_id=((me + o) % n, t), device_id_type=MESH)
    pl.semaphore_wait(barrier, n - 1)
    copies = []
    for o in range(1, n):
        copy = pltpu.make_async_remote_copy(
            src_ref=value, dst_ref=held.at[o],
            send_sem=send_sem.at[o], recv_sem=recv_sem.at[o],
            device_id=((me + o) % n, t), device_id_type=MESH,
        )
        copy.start()
        copies.append(copy)
    acc = value[...]
    for o, copy in zip(range(1, n), copies):
        copy.wait_recv()
        acc += held[o]
    total[...] = acc
    for copy in copies:
        copy.wait_send()


def sum_over_seq(n, value):
    vmem = pl.BlockSpec(memory_space=pltpu.VMEM)
    dma = pltpu.SemaphoreType.DMA
    return pl.pallas_call(
        functools.partial(sum_kernel, n),
        out_shape=jax.ShapeDtypeStruct(value.shape, value.dtype),
        in_specs=[vmem],
        out_specs=vmem,
        scratch_shapes=[pltpu.VMEM((n,) + value.shape, value.dtype), dma((n,)), dma((n,))],
        compiler_params=pltpu.CompilerParams(collective_id=1, has_side_effects=True),
    )(value)


def shards(
    teacher_rows,
    teacher_gain,
    teacher_counts,
    projector,
    student_rows,
    student_gain,
    span_shift,
    span_len,
    align_weights,
):
    n, tp = lax.axis_size("seq"), lax.axis_size("tp")
    me = lax.axis_index("seq")
    g = group_size(n)
    nq = n // g
    p, q = me % g, me // g
    teacher_width = teacher_rows.shape[1] * tp
    student_width = student_rows.shape[1] * tp
    capacity = teacher_rows.shape[0]
    rows_here = student_rows.shape[0]
    block_size = align_weights.shape[1]
    blocks = span_shift.shape[0]
    width = projector.shape[1]
    nl = nq // tp
    seq_rows = rows_here * n

    teacher_float = teacher_rows.astype(jnp.float32)
    squares = jnp.sum(teacher_float * teacher_float, axis=1)
    aux = jnp.concatenate(
        [squares, span_shift.astype(jnp.float32), span_len.astype(jnp.float32)]
    )
    aux_rows = -(-aux.shape[0] // 1024) * 8
    aux = jnp.pad(aux, (0, aux_rows * 128 - aux.shape[0])).reshape(aux_rows, 128)
    scaled = (projector.astype(jnp.float32) * teacher_gain[:, None]).astype(jnp.bfloat16)
    mapped, weights, aux_all = gather_map(g, nq, tp, teacher_rows, scaled, align_weights, aux)
    aux_all = aux_all.reshape(g, aux_rows * 128)
    square_sums = lax.psum(aux_all[:, :capacity], "tp")
    scales = lax.rsqrt(square_sums / teacher_width + epsilon)
    shifts = aux_all[:, capacity : capacity + blocks].astype(jnp.int32)
    lengths = aux_all[:, capacity + blocks : capacity + 2 * blocks].astype(jnp.int32)

    members = jnp.arange(g, dtype=jnp.int32)
    if g == 4:
        slot_of = jnp.bitwise_xor(members, p)
    else:
        slot_of = (p - members + g) % g
    mapped = mapped.reshape(nl, g, capacity, width)
    scale_slots = jnp.take(scales, slot_of, axis=0)
    mapped = (mapped.astype(jnp.float32) * scale_slots[None, :, :, None]).astype(jnp.bfloat16)

    starts = jnp.cumsum(teacher_counts) - teacher_counts
    low = block_size
    high = 2 * block_size - (2 * rows_here - capacity) // blocks
    last_count = jnp.take(teacher_counts, q * g + g - 1)
    tail = lax.dynamic_slice(
        mapped, (0, slot_of[g - 1], last_count - low, 0), (nl, 1, low, width)
    )[:, 0]
    head = lax.dynamic_slice(mapped, (0, slot_of[0], 0, 0), (nl, 1, high, width))[:, 0]
    below = lax.ppermute(tail, "seq", [(i, i + g) for i in range(n - g)])
    above = lax.ppermute(head, "seq", [(i + g, i) for i in range(n - g)])
    padded = jnp.concatenate([below, mapped.reshape(nl, g * capacity, width), above], axis=1)

    ids = q * g + members
    counts = jnp.take(teacher_counts, ids)
    own = jnp.take(starts, ids)
    block_ids = jnp.arange(blocks, dtype=jnp.int32)
    span = own[:, None] + block_ids[None, :] * counts[:, None] // blocks + shifts
    span = jnp.clip(span, 0, seq_rows - lengths)
    offsets = jnp.arange(block_size, dtype=jnp.int32)
    index = span[:, :, None] + offsets
    before = jnp.take(starts, jnp.maximum(ids - 1, 0))
    slot_before = jnp.take(slot_of, jnp.maximum(members - 1, 0))
    slot_after = jnp.take(slot_of, jnp.minimum(members + 1, g - 1))
    base_before = jnp.where(members == 0, low - own, low + slot_before * capacity - before)
    base_own = low + slot_of * capacity - own
    base_after = jnp.where(members == g - 1, low + g * capacity, low + slot_after * capacity) - (
        own + counts
    )
    wide = lambda v: v[:, None, None]
    slot = index + jnp.where(
        index < wide(own),
        wide(base_before),
        jnp.where(index < wide(own + counts), wide(base_own), wide(base_after)),
    )
    slot = jnp.clip(slot, 0, padded.shape[1] - 1)
    windows = jnp.take(padded, slot.reshape(-1), axis=1).reshape(
        nl, g * blocks, block_size, width
    )
    live = (offsets < lengths[:, :, None]).reshape(g * blocks, 1, block_size)
    weights = weights.reshape(g * blocks, block_size, block_size)
    weights = jnp.where(live, weights, jnp.zeros_like(weights))
    mixed = jnp.einsum("bij,zbjc->bizc", weights, windows, preferred_element_type=jnp.float32)
    mixed = mixed.astype(jnp.bfloat16).reshape(g, rows_here, nl, width)

    pieces = []
    for e in range(g):
        piece = lax.dynamic_index_in_dim(mixed, partner(p, e, g)[1], 0, keepdims=False)
        if e:
            hops = [(i, i // g * g + partner(i % g, e, g)[1]) for i in range(n)]
            piece = lax.ppermute(piece, "seq", hops)
        pieces.append(piece)
    target = jnp.take(jnp.stack(pieces), slot_of, axis=0)
    target = jnp.transpose(target, (1, 2, 0, 3)).reshape(rows_here, nl * g * width)
    target = target.astype(jnp.float32)

    student = student_rows.astype(jnp.float32)
    target_sums, student_sums = lax.psum(
        (jnp.sum(target * target, axis=1), jnp.sum(student * student, axis=1)), "tp"
    )
    target_hat = target * lax.rsqrt(target_sums / student_width + epsilon)[:, None]
    student_scale = lax.rsqrt(student_sums / student_width + epsilon)[:, None]
    student_hat = student * student_scale
    residual = student_hat * student_gain[None, :] - target_hat
    weighted = residual * student_gain[None, :]
    inner_sums = lax.psum(jnp.sum(weighted * student_hat, axis=1), "tp")
    inner_mean = (inner_sums / student_width)[:, None]
    row_grad = (student_scale * (weighted - student_hat * inner_mean)).astype(jnp.bfloat16)
    gain_terms = jnp.sum(residual * student_hat, axis=0)
    gain_grad = sum_over_seq(n, gain_terms.reshape(-1, 128)).reshape(-1) / seq_rows
    return (row_grad, gain_grad)


def solution(mesh):
    placed = (
        P("seq", "tp"),
        P("tp"),
        P(),
        P("tp", "seq"),
        P("seq", "tp"),
        P("tp"),
        P("seq"),
        P("seq"),
        P("seq", None),
    )
    return jax.shard_map(
        shards, mesh=mesh, in_specs=placed, out_specs=(P("seq", "tp"), P("tp")), check_vma=False
    )
```

```python
import functools

import jax
import jax.numpy as jnp
from jax import lax
from jax.experimental import pallas as pl
from jax.experimental.pallas import tpu as pltpu
from jax.sharding import PartitionSpec as P

epsilon = 1e-06
MESH = pl.DeviceIdType.MESH
VMEM_LIMIT = 52 * 1024 * 1024


def group_size(count):
    size = 1
    while size * size < count:
        size *= 2
    return size


def partner(p, e, g):
    if g == 4:
        if e == 0:
            return p, p
        low, high = 1 - 2 * (p % 2), 2 - 4 * (p // 2)
        other = p + (low if e % 2 else 0) + (high if e // 2 else 0)
        return other, other
    return (p - e + g) % g, (p + e) % g


def gather_kernel(
    g, nq, tp, nh,
    x_hbm, p_hbm, w_hbm, a_hbm,
    mapped, w_all, a_all,
    xs, ps, part, recv,
    x_send, x_recv, u_send, d_send, p_recv, s_send, s_recv, a_send, a_recv, t_send, t_recv, local,
):
    me, t = lax.axis_index("seq"), lax.axis_index("tp")
    p, q = me % g, me // g
    base = q * g
    half = xs.shape[1]
    nl = nq // tp

    barrier = pltpu.get_barrier_semaphore()
    n = g * nq
    for o in range(1, n):
        pl.semaphore_signal(barrier, inc=1, device_id=((me + o) % n, t), device_id_type=MESH)
    for o in range(1, tp):
        pl.semaphore_signal(barrier, inc=1, device_id=(me, (t + o) % tp), device_id_type=MESH)
    pl.semaphore_wait(barrier, n - 1 + tp - 1)

    def x_copy(source, e, h, member):
        return pltpu.make_async_remote_copy(
            src_ref=source, dst_ref=xs.at[e * nh + h],
            send_sem=x_send.at[e * nh + h], recv_sem=x_recv.at[e * nh + h],
            device_id=(base + member, t), device_id_type=MESH,
        )

    def own(h):
        return x_hbm.at[pl.ds(h * half, half)]

    def p_copy(source, block, sem, seq):
        return pltpu.make_async_remote_copy(
            src_ref=source, dst_ref=ps.at[block], send_sem=sem, recv_sem=p_recv.at[block],
            device_id=(seq, t), device_id_type=MESH,
        )

    relayed = g == 4
    direct = [1, 2] if relayed else list(range(1, g))

    def up(s):
        return p_copy(p_hbm if s == 0 else ps.at[q - s], q - s, u_send.at[s], me + g)

    def down(s):
        return p_copy(p_hbm if s == 0 else ps.at[q + s], q + s, d_send.at[s], me - g)

    def forward(s):
        @pl.when(q - s >= 0)
        def _():
            if s > 0:
                p_copy(p_hbm, q - s, u_send.at[0], me).wait_recv()

            @pl.when(q < nq - 1)
            def _():
                up(s).start()

        @pl.when(q + s < nq)
        def _():
            if s > 0:
                p_copy(p_hbm, q + s, u_send.at[0], me).wait_recv()

            @pl.when(q > 0)
            def _():
                down(s).start()

    first = []
    for h in range(nh):
        for e in direct:
            k = nh - 1 - h if e == 2 else h
            first.append((e, k))
    for e, h in first[: len(direct)]:
        x_copy(own(h), e, h, partner(p, e, g)[1]).start()
    forward(0)
    for e, h in first[len(direct):]:
        x_copy(own(h), e, h, partner(p, e, g)[1]).start()

    smalls = []
    for o in range(1, n):
        copy = pltpu.make_async_remote_copy(
            src_ref=a_hbm, dst_ref=a_all.at[me], send_sem=a_send.at[o], recv_sem=a_recv.at[o],
            device_id=((me + o) % n, t), device_id_type=MESH,
        )
        copy.start()
        smalls.append(copy)
    for e in range(1, g):
        copy = pltpu.make_async_remote_copy(
            src_ref=w_hbm, dst_ref=w_all.at[p], send_sem=s_send.at[e], recv_sem=s_recv.at[e],
            device_id=(base + (p + e) % g, t), device_id_type=MESH,
        )
        copy.start()
        smalls.append(copy)
    locals_ = [
        pltpu.make_async_copy(p_hbm, ps.at[q], local.at[0]),
        pltpu.make_async_copy(w_hbm, w_all.at[p], local.at[1]),
        pltpu.make_async_copy(a_hbm, a_all.at[me], local.at[2]),
    ]
    for h in range(nh):
        locals_.append(pltpu.make_async_copy(own(h), xs.at[h], local.at[3 + h]))
    for copy in locals_:
        copy.start()
    for copy in locals_:
        copy.wait()

    def multiply(c0, c1, b0, b1):
        def blocks(b, carry):
            def chunks(c, inner):
                part[b, c] = jnp.dot(
                    xs[c], ps[b], preferred_element_type=jnp.float32
                ).astype(jnp.bfloat16)
                return inner

            return lax.fori_loop(c0, c1, chunks, carry)

        lax.fori_loop(b0, b1, blocks, 0)

    def near(s):
        return jnp.maximum(q - s, 0), jnp.minimum(q + s, nq - 1) + 1

    def at_distance(s, c0, c1):
        @pl.when(q - s >= 0)
        def _():
            multiply(c0, c1, q - s, q - s + 1)

        @pl.when(q + s < nq)
        def _():
            multiply(c0, c1, q + s, q + s + 1)

    for e, h in first[: len(direct)]:
        copy = x_copy(own(h), e, h, partner(p, e, g)[1])
        copy.wait_recv()
        if relayed:
            x_copy(xs.at[e * nh + h], 3, h, partner(p, 3 - e, g)[1]).start()
    forward(1)
    for e, h in first[len(direct):]:
        x_copy(own(h), e, h, partner(p, e, g)[1]).wait_recv()
    early = (1 + len(direct)) * nh
    multiply(0, early, *near(1))
    for s in range(2, nq - 1):
        forward(s)
        at_distance(s, 0, early)
    if relayed:
        for h in range(nh):
            x_copy(xs.at[3 * nh + h], 3, h, p).wait_recv()
        multiply(early, g * nh, *near(nq - 2))
    forward(nq - 1)
    at_distance(nq - 1, 0, g * nh)

    sums = []
    for o in range(1, tp):
        other = (t + o) % tp
        copy = pltpu.make_async_remote_copy(
            src_ref=part.at[pl.ds(other * nl, nl)], dst_ref=recv.at[o - 1],
            send_sem=t_send.at[o - 1], recv_sem=t_recv.at[o - 1],
            device_id=(me, other), device_id_type=MESH,
        )
        copy.start()
        sums.append(copy)
    for copy in smalls + sums:
        copy.wait()

    def add(i, carry):
        block, chunk = i // (g * nh), i % (g * nh)
        total = part[t * nl + block, chunk].astype(jnp.float32)
        for o in range(1, tp):
            total += recv[o - 1, block, chunk].astype(jnp.float32)
        mapped[block, chunk] = total.astype(jnp.bfloat16)
        return carry

    lax.fori_loop(0, nl * g * nh, add, 0)

    for e, h in first:
        x_copy(own(h), e, h, partner(p, e, g)[1]).wait_send()
    if relayed:
        for e, h in first[: len(direct)]:
            x_copy(xs.at[e * nh + h], 3, h, partner(p, 3 - e, g)[1]).wait_send()
    for s in range(nq - 1):
        @pl.when((q - s >= 0) & (q < nq - 1))
        def _():
            up(s).wait_send()

        @pl.when((q + s < nq) & (q > 0))
        def _():
            down(s).wait_send()


def gather_map(g, nq, tp, x, p, w, a):
    rows, depth = x.shape
    width = p.shape[1]
    nh = 2 if rows % 32 == 0 else 1
    half = rows // nh
    nl = nq // tp
    any_spec = pl.BlockSpec(memory_space=pl.ANY)
    vmem = pl.BlockSpec(memory_space=pltpu.VMEM)
    dma = pltpu.SemaphoreType.DMA
    return pl.pallas_call(
        functools.partial(gather_kernel, g, nq, tp, nh),
        out_shape=(
            jax.ShapeDtypeStruct((nl, g * nh, half, width), jnp.bfloat16),
            jax.ShapeDtypeStruct((g,) + w.shape, w.dtype),
            jax.ShapeDtypeStruct((g * nq,) + a.shape, a.dtype),
        ),
        in_specs=[any_spec] * 4,
        out_specs=(vmem, vmem, vmem),
        scratch_shapes=[
            pltpu.VMEM((g * nh, half, depth), jnp.bfloat16),
            pltpu.VMEM((nq, depth, width), jnp.bfloat16),
            pltpu.VMEM((nq, g * nh, half, width), jnp.bfloat16),
            pltpu.VMEM((max(tp - 1, 1), nl, g * nh, half, width), jnp.bfloat16),
            dma((g * nh,)),
            dma((g * nh,)),
            dma((nq,)),
            dma((nq,)),
            dma((nq,)),
            dma((g,)),
            dma((g,)),
            dma((g * nq,)),
            dma((g * nq,)),
            dma((tp,)),
            dma((tp,)),
            dma((3 + nh,)),
        ],
        compiler_params=pltpu.CompilerParams(
            collective_id=0, has_side_effects=True, vmem_limit_bytes=VMEM_LIMIT
        ),
        cost_estimate=pl.CostEstimate(
            flops=2 * g * rows * depth * nq * width,
            bytes_accessed=2 * (g * rows * depth + nq * depth * width),
            transcendentals=0,
        ),
    )(x, p, w, a)


def mix_kernel(g, blocks, low, high, info, mapped, below, above, weights, mixed, held):
    nl, width = mapped.shape[0], mapped.shape[2]
    size = weights.shape[1]
    live = low + mapped.shape[1] + high
    for z in range(nl):
        columns = slice(z * width, (z + 1) * width)
        held[0:low, columns] = below[z]
        held[low : live - high, columns] = mapped[z]
        held[live - high : live, columns] = above[z]
    held[live:, :] = jnp.zeros((held.shape[0] - live, held.shape[1]), held.dtype)
    lanes = lax.broadcasted_iota(jnp.int32, (size, size), 1)

    def one(b, carry):
        cut = info[2 * g * blocks + b]
        source = weights[b].astype(jnp.float32)
        total = None
        for part in range(2):
            start = info[part * g * blocks + b]
            kept = jnp.where((lanes < cut) if part == 0 else (lanes >= cut), source, 0.0)
            spread = jnp.concatenate([kept, jnp.zeros_like(kept)], axis=1)
            spread = pltpu.roll(spread, start % 16, axis=1).astype(jnp.bfloat16)
            rows = held[pl.ds(pl.multiple_of(start // 16 * 16, 16), 2 * size), :]
            product = jnp.dot(spread, rows, preferred_element_type=jnp.float32)
            total = product if total is None else total + product
        mixed[b] = total.astype(jnp.bfloat16)
        return carry

    lax.fori_loop(0, g * blocks, one, 0)


def mix(g, blocks, info, mapped, below, above, weights):
    nl, span_rows, width = mapped.shape
    low, high, size = below.shape[1], above.shape[1], weights.shape[1]
    vmem = pl.BlockSpec(memory_space=pltpu.VMEM)
    return pl.pallas_call(
        functools.partial(mix_kernel, g, blocks, low, high),
        out_shape=jax.ShapeDtypeStruct((g * blocks, size, nl * width), jnp.bfloat16),
        in_specs=[pl.BlockSpec(memory_space=pltpu.SMEM)] + [vmem] * 4,
        out_specs=vmem,
        scratch_shapes=[
            pltpu.VMEM((low + span_rows + high + 2 * size, nl * width), jnp.bfloat16)
        ],
        compiler_params=pltpu.CompilerParams(vmem_limit_bytes=VMEM_LIMIT),
    )(info, mapped, below, above, weights)


def finish_kernel(
    g, n, tp, nl, width, student_width, step,
    mixed, student, gain, row_grad, gain_grad,
    target, sums, sums_in, terms, gained, gained_in,
    m_send, m_recv, t_send, t_recv, g_send, g_recv,
):
    me, t = lax.axis_index("seq"), lax.axis_index("tp")
    p = me % g
    base = me - p
    rows = student.shape[0]
    barrier = pltpu.get_barrier_semaphore()
    for o in range(1, n):
        pl.semaphore_signal(barrier, inc=1, device_id=((me + o) % n, t), device_id_type=MESH)
    for o in range(1, tp):
        pl.semaphore_signal(barrier, inc=1, device_id=(me, (t + o) % tp), device_id_type=MESH)
    pl.semaphore_wait(barrier, n - 1 + tp - 1)

    copies = []
    for e in range(1, g):
        member = partner(p, e, g)[1]
        copy = pltpu.make_async_remote_copy(
            src_ref=mixed.at[member], dst_ref=target.at[p],
            send_sem=m_send.at[e], recv_sem=m_recv.at[e],
            device_id=(base + member, t), device_id_type=MESH,
        )
        copy.start()
        copies.append(copy)
    own = pltpu.make_async_copy(mixed.at[p], target.at[p], m_send.at[0])
    own.start()
    own.wait()
    for copy in copies:
        copy.wait_recv()

    tiles = [(m, z) for z in range(nl) for m in range(g)]

    def load(r, m, z):
        here = pl.ds(pl.multiple_of(r * step, step), step)
        start = (z * g + m) * width
        s = student[here, start : start + width].astype(jnp.float32)
        v = target[m, here, z * width : (z + 1) * width].astype(jnp.float32)
        return s, v, gain[:, start : start + width]

    lanes = lax.broadcasted_iota(jnp.int32, (step, 128), 1)

    def count(r, carry):
        parts = [0.0] * 4
        for m, z in tiles:
            s, v, gn = load(r, m, z)
            sg = s * gn
            for k, term in enumerate((s * s, sg * sg, v * v, sg * v)):
                parts[k] = parts[k] + term
        packed = jnp.zeros((step, 128), jnp.float32)
        for k in range(4):
            packed = jnp.where(lanes == k, jnp.sum(parts[k], axis=1, keepdims=True), packed)
        sums[pl.ds(pl.multiple_of(r * step, step), step), :] = packed
        return carry

    lax.fori_loop(0, rows // step, count, 0)

    pairs = []
    for o in range(1, tp):
        copy = pltpu.make_async_remote_copy(
            src_ref=sums, dst_ref=sums_in.at[o - 1],
            send_sem=t_send.at[o - 1], recv_sem=t_recv.at[o - 1],
            device_id=(me, (t + o) % tp), device_id_type=MESH,
        )
        copy.start()
        pairs.append(copy)
    for copy in pairs:
        copy.wait_recv()

    terms[...] = jnp.zeros_like(terms)

    def grade(r, carry):
        here = pl.ds(pl.multiple_of(r * step, step), step)
        total = sums[here, :]
        for o in range(1, tp):
            total += sums_in[o - 1, here, :]
        ss, gg, vv, sv = [total[:, k : k + 1] for k in range(4)]
        s_scale = lax.rsqrt(ss / student_width + epsilon)
        v_scale = lax.rsqrt(vv / student_width + epsilon)
        inner = (s_scale * s_scale * gg - s_scale * v_scale * sv) / student_width
        for m, z in tiles:
            s, v, gn = load(r, m, z)
            start = (z * g + m) * width
            hat = s * s_scale
            residual = hat * gn - v * v_scale
            out = s_scale * (residual * gn - hat * inner)
            row_grad[here, start : start + width] = out.astype(row_grad.dtype)
            product = residual * hat
            terms[:, start : start + width] += sum(
                product[8 * i : 8 * i + 8] for i in range(step // 8)
            )
        return carry

    lax.fori_loop(0, rows // step, grade, 0)

    gained[...] = jnp.sum(terms[...], axis=0, keepdims=True)
    lasts = []
    for o in range(1, n):
        copy = pltpu.make_async_remote_copy(
            src_ref=gained, dst_ref=gained_in.at[o],
            send_sem=g_send.at[o], recv_sem=g_recv.at[o],
            device_id=((me + o) % n, t), device_id_type=MESH,
        )
        copy.start()
        lasts.append(copy)
    total = gained[...]
    for o, copy in zip(range(1, n), lasts):
        copy.wait_recv()
        total += gained_in[o]
    gain_grad[...] = total / (rows * n)
    for copy in copies + pairs + lasts:
        copy.wait_send()


def finish(g, n, tp, mixed, student, gain, width):
    rows, columns = student.shape
    nl = mixed.shape[2] // width
    vmem = pl.BlockSpec(memory_space=pltpu.VMEM)
    dma = pltpu.SemaphoreType.DMA
    step = 32 if rows % 32 == 0 else 16
    return pl.pallas_call(
        functools.partial(finish_kernel, g, n, tp, nl, width, columns * tp, step),
        out_shape=(
            jax.ShapeDtypeStruct((rows, columns), jnp.bfloat16),
            jax.ShapeDtypeStruct((1, columns), jnp.float32),
        ),
        in_specs=[vmem] * 3,
        out_specs=(vmem, vmem),
        scratch_shapes=[
            pltpu.VMEM(mixed.shape, mixed.dtype),
            pltpu.VMEM((rows, 128), jnp.float32),
            pltpu.VMEM((max(tp - 1, 1), rows, 128), jnp.float32),
            pltpu.VMEM((8, columns), jnp.float32),
            pltpu.VMEM((1, columns), jnp.float32),
            pltpu.VMEM((n, 1, columns), jnp.float32),
            dma((g,)),
            dma((g,)),
            dma((tp,)),
            dma((tp,)),
            dma((n,)),
            dma((n,)),
        ],
        compiler_params=pltpu.CompilerParams(
            collective_id=1, has_side_effects=True, vmem_limit_bytes=VMEM_LIMIT
        ),
    )(mixed, student, gain)


def shards(
    teacher_rows,
    teacher_gain,
    teacher_counts,
    projector,
    student_rows,
    student_gain,
    span_shift,
    span_len,
    align_weights,
):
    n, tp = lax.axis_size("seq"), lax.axis_size("tp")
    me = lax.axis_index("seq")
    g = group_size(n)
    nq = n // g
    p, q = me % g, me // g
    teacher_width = teacher_rows.shape[1] * tp
    student_width = student_rows.shape[1] * tp
    capacity = teacher_rows.shape[0]
    rows_here = student_rows.shape[0]
    block_size = align_weights.shape[1]
    blocks = span_shift.shape[0]
    width = projector.shape[1]
    nl = nq // tp
    seq_rows = rows_here * n

    teacher_float = teacher_rows.astype(jnp.float32)
    squares = jnp.sum(teacher_float * teacher_float, axis=1)
    aux = jnp.concatenate(
        [squares, span_shift.astype(jnp.float32), span_len.astype(jnp.float32)]
    )
    aux_rows = -(-aux.shape[0] // 1024) * 8
    aux = jnp.pad(aux, (0, aux_rows * 128 - aux.shape[0])).reshape(aux_rows, 128)
    scaled = (projector.astype(jnp.float32) * teacher_gain[:, None]).astype(jnp.bfloat16)
    mapped, weights, aux_all = gather_map(g, nq, tp, teacher_rows, scaled, align_weights, aux)
    aux_all = aux_all.reshape(n, aux_rows * 128)
    square_sums = lax.psum(aux_all[:, :capacity], "tp")
    scales = lax.rsqrt(square_sums / teacher_width + epsilon)
    spans = lax.dynamic_slice(aux_all, (q * g, capacity), (g, 2 * blocks)).astype(jnp.int32)
    shifts, lengths = spans[:, :blocks], spans[:, blocks:]

    members = jnp.arange(g, dtype=jnp.int32)
    if g == 4:
        slot_of = jnp.bitwise_xor(members, p)
    else:
        slot_of = (p - members + g) % g
    mapped = mapped.reshape(nl, g * capacity, width)

    starts = jnp.cumsum(teacher_counts) - teacher_counts
    low = block_size
    high = 2 * block_size - (2 * rows_here - capacity) // blocks
    last_count = jnp.take(teacher_counts, q * g + g - 1)
    tail_at = slot_of[g - 1] * capacity + last_count - low
    tail = lax.dynamic_slice(mapped, (0, tail_at, 0), (nl, low, width))
    head = lax.dynamic_slice(mapped, (0, slot_of[0] * capacity, 0), (nl, high, width))
    below = lax.ppermute(tail, "seq", [(i, i + g) for i in range(n - g)])
    above = lax.ppermute(head, "seq", [(i + g, i) for i in range(n - g)])

    ids = q * g + members
    counts = lax.dynamic_slice(teacher_counts, (q * g,), (g,))
    own = lax.dynamic_slice(starts, (q * g,), (g,))
    after = own + counts
    block_ids = jnp.arange(blocks, dtype=jnp.int32)
    span = own[:, None] + block_ids[None, :] * counts[:, None] // blocks + shifts
    span = jnp.clip(span, 0, seq_rows - lengths)
    before = own - jnp.concatenate([counts[:1], counts[:-1]])
    slot_rows = low + slot_of * capacity
    base_before = jnp.where(
        members == 0, low - own, jnp.concatenate([slot_rows[:1], slot_rows[:-1]]) - before
    )
    base_own = slot_rows - own
    base_after = (
        jnp.where(
            members == g - 1,
            low + g * capacity,
            jnp.concatenate([slot_rows[1:], slot_rows[-1:]]),
        )
        - after
    )
    is_before = span < own[:, None]
    is_own = span < after[:, None]
    first_base = jnp.where(
        is_before, base_before[:, None], jnp.where(is_own, base_own[:, None], base_after[:, None])
    )
    second_base = jnp.where(is_before, base_own[:, None], base_after[:, None])
    cut = jnp.where(
        is_before, own[:, None] - span, jnp.where(is_own, after[:, None] - span, block_size)
    )
    cut = jnp.minimum(cut, block_size)
    last_start = low + g * capacity + high
    first_start = jnp.clip(span + first_base, 0, last_start)
    second_start = jnp.clip(span + second_base, 0, last_start)
    info = jnp.concatenate(
        [first_start.reshape(-1), second_start.reshape(-1), cut.reshape(-1)]
    ).astype(jnp.int32)

    offsets = jnp.arange(block_size, dtype=jnp.int32)
    index = span[:, :, None] + offsets
    owner = ids[:, None, None] + jnp.where(
        index < own[:, None, None], -1, jnp.where(index < after[:, None, None], 0, 1)
    )
    owner = jnp.clip(owner, 0, n - 1)
    row = jnp.clip(index - jnp.take(starts, owner), 0, capacity - 1)
    window_scales = jnp.take(scales.reshape(-1), owner * capacity + row)
    window_scales = jnp.where(offsets < lengths[:, :, None], window_scales, 0.0)
    weights = weights.reshape(g * blocks, block_size, block_size).astype(jnp.float32)
    weights = weights * window_scales.reshape(g * blocks, 1, block_size)
    mixed = mix(g, blocks, info, mapped, below, above, weights.astype(jnp.bfloat16))
    row_grad, gain_grad = finish(
        g, n, tp, mixed.reshape(g, rows_here, nl * width), student_rows, student_gain[None, :], width
    )
    return (row_grad, gain_grad.reshape(-1))


def solution(mesh):
    placed = (
        P("seq", "tp"),
        P("tp"),
        P(),
        P("tp", "seq"),
        P("seq", "tp"),
        P("tp"),
        P("seq"),
        P("seq"),
        P("seq", None),
    )
    return jax.shard_map(
        shards, mesh=mesh, in_specs=placed, out_specs=(P("seq", "tp"), P("tp")), check_vma=False
    )
```

```python
import functools

import jax
import jax.numpy as jnp
from jax import lax
from jax.experimental import pallas as pl
from jax.experimental.pallas import tpu as pltpu
from jax.sharding import PartitionSpec as P

epsilon = 1e-06
MESH = pl.DeviceIdType.MESH
VMEM_LIMIT = 52 * 1024 * 1024


def group_size(count):
    size = 1
    while size * size < count:
        size *= 2
    return size


def partner(p, e, g):
    if g == 4:
        if e == 0:
            return p, p
        low, high = 1 - 2 * (p % 2), 2 - 4 * (p // 2)
        other = p + (low if e % 2 else 0) + (high if e // 2 else 0)
        return other, other
    return (p - e + g) % g, (p + e) % g


def gather_kernel(
    g, nq, tp, nh, np_,
    x_hbm, p_hbm, w_hbm, a_hbm,
    mapped, w_all, a_all,
    xs, ps, part, recv,
    x_send, x_recv, u_send, d_send, p_recv, s_send, s_recv, a_send, a_recv, t_send, t_recv, local,
):
    me, t = lax.axis_index("seq"), lax.axis_index("tp")
    p, q = me % g, me // g
    base = q * g
    half = xs.shape[1]
    nl = nq // tp

    barrier = pltpu.get_barrier_semaphore()
    n = g * nq
    for o in range(1, n):
        pl.semaphore_signal(barrier, inc=1, device_id=((me + o) % n, t), device_id_type=MESH)
    for o in range(1, tp):
        pl.semaphore_signal(barrier, inc=1, device_id=(me, (t + o) % tp), device_id_type=MESH)
    pl.semaphore_wait(barrier, n - 1 + tp - 1)

    def x_copy(source, e, h, member):
        return pltpu.make_async_remote_copy(
            src_ref=source, dst_ref=xs.at[e * nh + h],
            send_sem=x_send.at[e * nh + h], recv_sem=x_recv.at[e * nh + h],
            device_id=(base + member, t), device_id_type=MESH,
        )

    def own(h):
        return x_hbm.at[pl.ds(h * half, half)]

    piece = p_hbm.shape[0] // np_

    def p_copy(source, block, k, sem, seq):
        return pltpu.make_async_remote_copy(
            src_ref=source, dst_ref=ps.at[block, pl.ds(k * piece, piece)],
            send_sem=sem, recv_sem=p_recv.at[block * np_ + k],
            device_id=(seq, t), device_id_type=MESH,
        )

    relayed = g == 4
    direct = [1, 2] if relayed else list(range(1, g))

    def held(s, block, k):
        here = pl.ds(k * piece, piece)
        return p_hbm.at[here] if s == 0 else ps.at[block, here]

    def up(s, k):
        return p_copy(held(s, q - s, k), q - s, k, u_send.at[s * np_ + k], me + g)

    def down(s, k):
        return p_copy(held(s, q + s, k), q + s, k, d_send.at[s * np_ + k], me - g)

    def forward(s, k):
        @pl.when(q - s >= 0)
        def _():
            if s > 0:
                p_copy(held(0, q, k), q - s, k, u_send.at[0], me).wait_recv()

            @pl.when(q < nq - 1)
            def _():
                up(s, k).start()

        @pl.when(q + s < nq)
        def _():
            if s > 0:
                p_copy(held(0, q, k), q + s, k, u_send.at[0], me).wait_recv()

            @pl.when(q > 0)
            def _():
                down(s, k).start()

    first = []
    for h in range(nh):
        for e in direct:
            k = nh - 1 - h if e == 2 else h
            first.append((e, k))
    for e, h in first[: len(direct)]:
        x_copy(own(h), e, h, partner(p, e, g)[1]).start()
    for k in range(np_):
        forward(0, k)
    for e, h in first[len(direct):]:
        x_copy(own(h), e, h, partner(p, e, g)[1]).start()

    smalls = []
    for o in range(1, n):
        copy = pltpu.make_async_remote_copy(
            src_ref=a_hbm, dst_ref=a_all.at[me], send_sem=a_send.at[o], recv_sem=a_recv.at[o],
            device_id=((me + o) % n, t), device_id_type=MESH,
        )
        copy.start()
        smalls.append(copy)
    for e in range(1, g):
        copy = pltpu.make_async_remote_copy(
            src_ref=w_hbm, dst_ref=w_all.at[p], send_sem=s_send.at[e], recv_sem=s_recv.at[e],
            device_id=(base + (p + e) % g, t), device_id_type=MESH,
        )
        copy.start()
        smalls.append(copy)
    locals_ = [
        pltpu.make_async_copy(p_hbm, ps.at[q], local.at[0]),
        pltpu.make_async_copy(w_hbm, w_all.at[p], local.at[1]),
        pltpu.make_async_copy(a_hbm, a_all.at[me], local.at[2]),
    ]
    for h in range(nh):
        locals_.append(pltpu.make_async_copy(own(h), xs.at[h], local.at[3 + h]))
    for copy in locals_:
        copy.start()
    for copy in locals_:
        copy.wait()

    def multiply(c0, c1, b0, b1):
        def blocks(b, carry):
            def chunks(c, inner):
                part[b, c] = jnp.dot(
                    xs[c], ps[b], preferred_element_type=jnp.float32
                ).astype(jnp.bfloat16)
                return inner

            return lax.fori_loop(c0, c1, chunks, carry)

        lax.fori_loop(b0, b1, blocks, 0)

    def near(s):
        return jnp.maximum(q - s, 0), jnp.minimum(q + s, nq - 1) + 1

    def at_distance(s, c0, c1):
        @pl.when(q - s >= 0)
        def _():
            multiply(c0, c1, q - s, q - s + 1)

        @pl.when(q + s < nq)
        def _():
            multiply(c0, c1, q + s, q + s + 1)

    forward(1, 0)
    for e, h in first[: len(direct)]:
        x_copy(own(h), e, h, partner(p, e, g)[1]).wait_recv()
        if relayed:
            x_copy(xs.at[e * nh + h], 3, h, partner(p, 3 - e, g)[1]).start()
    for k in range(1, np_):
        forward(1, k)
    far = nq - 1
    for s in range(2, far):
        forward(s, 0)
    for e, h in first[len(direct):]:
        x_copy(own(h), e, h, partner(p, e, g)[1]).wait_recv()
    for s in range(2, far):
        for k in range(1, np_):
            forward(s, k)
    early = (1 + len(direct)) * nh
    multiply(0, early, *near(far - 1))
    if relayed:
        for h in range(nh):
            x_copy(xs.at[3 * nh + h], 3, h, p).wait_recv()
        multiply(early, g * nh, *near(far - 1))

    def sum_copy(o, j):
        other = (t + o) % tp
        return pltpu.make_async_remote_copy(
            src_ref=part.at[other * nl + j], dst_ref=recv.at[o - 1, j],
            send_sem=t_send.at[(o - 1) * nl + j], recv_sem=t_recv.at[(o - 1) * nl + j],
            device_id=(me, other), device_id_type=MESH,
        )

    def is_far(o, j):
        distance = (t + o) % tp * nl + j - q
        return (distance == far) | (distance == -far)

    sums = [(o, j) for o in range(1, tp) for j in range(nl)]
    for o, j in sums:
        @pl.when(jnp.logical_not(is_far(o, j)))
        def _():
            sum_copy(o, j).start()

    for k in range(np_):
        forward(far, k)
    at_distance(far, 0, g * nh)
    for o, j in sums:
        @pl.when(is_far(o, j))
        def _():
            sum_copy(o, j).start()

    for copy in smalls:
        copy.wait()
    for o, j in sums:
        sum_copy(o, j).wait_recv()

    def add(i, carry):
        block, chunk = i // (g * nh), i % (g * nh)
        total = part[t * nl + block, chunk].astype(jnp.float32)
        for o in range(1, tp):
            total += recv[o - 1, block, chunk].astype(jnp.float32)
        mapped[block, chunk] = total.astype(jnp.bfloat16)
        return carry

    lax.fori_loop(0, nl * g * nh, add, 0)

    for o, j in sums:
        sum_copy(o, j).wait_send()
    for e, h in first:
        x_copy(own(h), e, h, partner(p, e, g)[1]).wait_send()
    if relayed:
        for e, h in first[: len(direct)]:
            x_copy(xs.at[e * nh + h], 3, h, partner(p, 3 - e, g)[1]).wait_send()
    for s in range(nq - 1):
        @pl.when((q - s >= 0) & (q < nq - 1))
        def _():
            for k in range(np_):
                up(s, k).wait_send()

        @pl.when((q + s < nq) & (q > 0))
        def _():
            for k in range(np_):
                down(s, k).wait_send()


def gather_map(g, nq, tp, x, p, w, a):
    rows, depth = x.shape
    width = p.shape[1]
    nh = 2 if rows % 32 == 0 else 1
    half = rows // nh
    np_ = 2
    nl = nq // tp
    any_spec = pl.BlockSpec(memory_space=pl.ANY)
    vmem = pl.BlockSpec(memory_space=pltpu.VMEM)
    dma = pltpu.SemaphoreType.DMA
    return pl.pallas_call(
        functools.partial(gather_kernel, g, nq, tp, nh, np_),
        out_shape=(
            jax.ShapeDtypeStruct((nl, g * nh, half, width), jnp.bfloat16),
            jax.ShapeDtypeStruct((g,) + w.shape, w.dtype),
            jax.ShapeDtypeStruct((g * nq,) + a.shape, a.dtype),
        ),
        in_specs=[any_spec] * 4,
        out_specs=(vmem, vmem, vmem),
        scratch_shapes=[
            pltpu.VMEM((g * nh, half, depth), jnp.bfloat16),
            pltpu.VMEM((nq, depth, width), jnp.bfloat16),
            pltpu.VMEM((nq, g * nh, half, width), jnp.bfloat16),
            pltpu.VMEM((max(tp - 1, 1), nl, g * nh, half, width), jnp.bfloat16),
            dma((g * nh,)),
            dma((g * nh,)),
            dma((nq * np_,)),
            dma((nq * np_,)),
            dma((nq * np_,)),
            dma((g,)),
            dma((g,)),
            dma((g * nq,)),
            dma((g * nq,)),
            dma((tp * nl,)),
            dma((tp * nl,)),
            dma((3 + nh,)),
        ],
        compiler_params=pltpu.CompilerParams(
            collective_id=0, has_side_effects=True, vmem_limit_bytes=VMEM_LIMIT
        ),
        cost_estimate=pl.CostEstimate(
            flops=2 * g * rows * depth * nq * width,
            bytes_accessed=2 * (g * rows * depth + nq * depth * width),
            transcendentals=0,
        ),
    )(x, p, w, a)


def mix_kernel(g, blocks, low, high, info, scales, mapped, below, above, weights, mixed, held):
    nl, width = mapped.shape[0], mapped.shape[2]
    size = weights.shape[1]
    live = low + mapped.shape[1] + high
    for z in range(nl):
        columns = slice(z * width, (z + 1) * width)
        held[0:low, columns] = below[z]
        held[low : live - high, columns] = mapped[z]
        held[live - high : live, columns] = above[z]
    held[live:, :] = jnp.zeros((held.shape[0] - live, held.shape[1]), held.dtype)
    lanes = lax.broadcasted_iota(jnp.int32, (size, size), 1)

    def one(b, carry):
        cut, length = info[2 * g * blocks + b], info[3 * g * blocks + b]
        source = jnp.where(lanes < length, weights[b].astype(jnp.float32), 0.0)
        total = None
        for part in range(2):
            start = info[part * g * blocks + b]
            kept = jnp.where((lanes < cut) if part == 0 else (lanes >= cut), source, 0.0)
            spread = jnp.concatenate([kept, jnp.zeros_like(kept)], axis=1)
            spread = pltpu.roll(spread, start % size, axis=1)
            tile = start // size
            scale = jnp.concatenate([scales[tile], scales[tile + 1]], axis=1)
            spread = (spread * scale).astype(jnp.bfloat16)
            rows = held[pl.ds(pl.multiple_of(tile * size, size), 2 * size), :]
            product = jnp.dot(spread, rows, preferred_element_type=jnp.float32)
            total = product if total is None else total + product
        mixed[b] = total.astype(jnp.bfloat16)
        return carry

    lax.fori_loop(0, g * blocks, one, 0)


def mix(g, blocks, info, scales, mapped, below, above, weights):
    nl, span_rows, width = mapped.shape
    low, high, size = below.shape[1], above.shape[1], weights.shape[1]
    vmem = pl.BlockSpec(memory_space=pltpu.VMEM)
    return pl.pallas_call(
        functools.partial(mix_kernel, g, blocks, low, high),
        out_shape=jax.ShapeDtypeStruct((g * blocks, size, nl * width), jnp.bfloat16),
        in_specs=[pl.BlockSpec(memory_space=pltpu.SMEM)] + [vmem] * 5,
        out_specs=vmem,
        scratch_shapes=[
            pltpu.VMEM((low + span_rows + high + 2 * size, nl * width), jnp.bfloat16)
        ],
        compiler_params=pltpu.CompilerParams(vmem_limit_bytes=VMEM_LIMIT),
    )(info, scales, mapped, below, above, weights)


def finish_kernel(
    g, n, tp, nl, width, student_width, step,
    mixed, student, gain, row_grad, gain_grad,
    target, sums, sums_in, terms, gained, gained_in,
    m_send, m_recv, t_send, t_recv, g_send, g_recv,
):
    me, t = lax.axis_index("seq"), lax.axis_index("tp")
    p = me % g
    base = me - p
    rows = student.shape[0]
    barrier = pltpu.get_barrier_semaphore()
    for o in range(1, n):
        pl.semaphore_signal(barrier, inc=1, device_id=((me + o) % n, t), device_id_type=MESH)
    for o in range(1, tp):
        pl.semaphore_signal(barrier, inc=1, device_id=(me, (t + o) % tp), device_id_type=MESH)
    pl.semaphore_wait(barrier, n - 1 + tp - 1)

    copies = []
    for e in range(1, g):
        member = partner(p, e, g)[1]
        copy = pltpu.make_async_remote_copy(
            src_ref=mixed.at[member], dst_ref=target.at[p],
            send_sem=m_send.at[e], recv_sem=m_recv.at[e],
            device_id=(base + member, t), device_id_type=MESH,
        )
        copy.start()
        copies.append(copy)
    own = pltpu.make_async_copy(mixed.at[p], target.at[p], m_send.at[0])
    own.start()
    own.wait()
    for copy in copies:
        copy.wait_recv()

    tiles = [(m, z) for z in range(nl) for m in range(g)]

    def load(r, m, z):
        here = pl.ds(pl.multiple_of(r * step, step), step)
        start = (z * g + m) * width
        s = student[here, start : start + width].astype(jnp.float32)
        v = target[m, here, z * width : (z + 1) * width].astype(jnp.float32)
        return s, v, gain[:, start : start + width]

    lanes = lax.broadcasted_iota(jnp.int32, (step, 128), 1)

    def count(r, carry):
        parts = [0.0] * 4
        for m, z in tiles:
            s, v, gn = load(r, m, z)
            sg = s * gn
            for k, term in enumerate((s * s, sg * sg, v * v, sg * v)):
                parts[k] = parts[k] + term
        packed = jnp.zeros((step, 128), jnp.float32)
        for k in range(4):
            packed = jnp.where(lanes == k, jnp.sum(parts[k], axis=1, keepdims=True), packed)
        sums[pl.ds(pl.multiple_of(r * step, step), step), :] = packed
        return carry

    lax.fori_loop(0, rows // step, count, 0)

    pairs = []
    for o in range(1, tp):
        copy = pltpu.make_async_remote_copy(
            src_ref=sums, dst_ref=sums_in.at[o - 1],
            send_sem=t_send.at[o - 1], recv_sem=t_recv.at[o - 1],
            device_id=(me, (t + o) % tp), device_id_type=MESH,
        )
        copy.start()
        pairs.append(copy)
    for copy in pairs:
        copy.wait_recv()

    terms[...] = jnp.zeros_like(terms)

    def grade(r, carry):
        here = pl.ds(pl.multiple_of(r * step, step), step)
        total = sums[here, :]
        for o in range(1, tp):
            total += sums_in[o - 1, here, :]
        ss, gg, vv, sv = [total[:, k : k + 1] for k in range(4)]
        s_scale = lax.rsqrt(ss / student_width + epsilon)
        v_scale = lax.rsqrt(vv / student_width + epsilon)
        inner = (s_scale * s_scale * gg - s_scale * v_scale * sv) / student_width
        for m, z in tiles:
            s, v, gn = load(r, m, z)
            start = (z * g + m) * width
            hat = s * s_scale
            residual = hat * gn - v * v_scale
            out = s_scale * (residual * gn - hat * inner)
            row_grad[here, start : start + width] = out.astype(row_grad.dtype)
            product = residual * hat
            terms[:, start : start + width] += sum(
                product[8 * i : 8 * i + 8] for i in range(step // 8)
            )
        return carry

    lax.fori_loop(0, rows // step, grade, 0)

    gained[...] = jnp.sum(terms[...], axis=0, keepdims=True)
    lasts = []
    for o in range(1, n):
        copy = pltpu.make_async_remote_copy(
            src_ref=gained, dst_ref=gained_in.at[o],
            send_sem=g_send.at[o], recv_sem=g_recv.at[o],
            device_id=((me + o) % n, t), device_id_type=MESH,
        )
        copy.start()
        lasts.append(copy)
    total = gained[...]
    for o, copy in zip(range(1, n), lasts):
        copy.wait_recv()
        total += gained_in[o]
    gain_grad[...] = total / (rows * n)
    for copy in copies + pairs + lasts:
        copy.wait_send()


def finish(g, n, tp, mixed, student, gain, width):
    rows, columns = student.shape
    nl = mixed.shape[2] // width
    vmem = pl.BlockSpec(memory_space=pltpu.VMEM)
    dma = pltpu.SemaphoreType.DMA
    step = 32 if rows % 32 == 0 else 16
    return pl.pallas_call(
        functools.partial(finish_kernel, g, n, tp, nl, width, columns * tp, step),
        out_shape=(
            jax.ShapeDtypeStruct((rows, columns), jnp.bfloat16),
            jax.ShapeDtypeStruct((1, columns), jnp.float32),
        ),
        in_specs=[vmem] * 3,
        out_specs=(vmem, vmem),
        scratch_shapes=[
            pltpu.VMEM(mixed.shape, mixed.dtype),
            pltpu.VMEM((rows, 128), jnp.float32),
            pltpu.VMEM((max(tp - 1, 1), rows, 128), jnp.float32),
            pltpu.VMEM((8, columns), jnp.float32),
            pltpu.VMEM((1, columns), jnp.float32),
            pltpu.VMEM((n, 1, columns), jnp.float32),
            dma((g,)),
            dma((g,)),
            dma((tp,)),
            dma((tp,)),
            dma((n,)),
            dma((n,)),
        ],
        compiler_params=pltpu.CompilerParams(
            collective_id=1, has_side_effects=True, vmem_limit_bytes=VMEM_LIMIT
        ),
    )(mixed, student, gain)


def shards(
    teacher_rows,
    teacher_gain,
    teacher_counts,
    projector,
    student_rows,
    student_gain,
    span_shift,
    span_len,
    align_weights,
):
    n, tp = lax.axis_size("seq"), lax.axis_size("tp")
    me = lax.axis_index("seq")
    g = group_size(n)
    nq = n // g
    p, q = me % g, me // g
    teacher_width = teacher_rows.shape[1] * tp
    student_width = student_rows.shape[1] * tp
    capacity = teacher_rows.shape[0]
    rows_here = student_rows.shape[0]
    block_size = align_weights.shape[1]
    blocks = span_shift.shape[0]
    width = projector.shape[1]
    nl = nq // tp
    seq_rows = rows_here * n

    teacher_float = teacher_rows.astype(jnp.float32)
    squares = jnp.sum(teacher_float * teacher_float, axis=1)
    aux = jnp.concatenate(
        [squares, span_shift.astype(jnp.float32), span_len.astype(jnp.float32)]
    )
    aux_rows = -(-aux.shape[0] // 1024) * 8
    aux = jnp.pad(aux, (0, aux_rows * 128 - aux.shape[0])).reshape(aux_rows, 128)
    scaled = (projector.astype(jnp.float32) * teacher_gain[:, None]).astype(jnp.bfloat16)
    mapped, weights, aux_all = gather_map(g, nq, tp, teacher_rows, scaled, align_weights, aux)
    aux_all = aux_all.reshape(n, aux_rows * 128)
    square_sums = lax.psum(aux_all[:, :capacity], "tp")
    scales = lax.rsqrt(square_sums / teacher_width + epsilon)
    spans = lax.dynamic_slice(aux_all, (q * g, capacity), (g, 2 * blocks)).astype(jnp.int32)
    shifts, lengths = spans[:, :blocks], spans[:, blocks:]

    members = jnp.arange(g, dtype=jnp.int32)
    if g == 4:
        slot_of = jnp.bitwise_xor(members, p)
    else:
        slot_of = (p - members + g) % g
    mapped = mapped.reshape(nl, g * capacity, width)

    starts = jnp.cumsum(teacher_counts) - teacher_counts
    low = block_size
    high = 2 * block_size - (2 * rows_here - capacity) // blocks
    last_count = jnp.take(teacher_counts, q * g + g - 1)
    tail_at = slot_of[g - 1] * capacity + last_count - low
    tail = lax.dynamic_slice(mapped, (0, tail_at, 0), (nl, low, width))
    head = lax.dynamic_slice(mapped, (0, slot_of[0] * capacity, 0), (nl, high, width))
    below = lax.ppermute(tail, "seq", [(i, i + g) for i in range(n - g)])
    above = lax.ppermute(head, "seq", [(i + g, i) for i in range(n - g)])

    ids = q * g + members
    counts = lax.dynamic_slice(teacher_counts, (q * g,), (g,))
    own = lax.dynamic_slice(starts, (q * g,), (g,))
    after = own + counts
    block_ids = jnp.arange(blocks, dtype=jnp.int32)
    span = own[:, None] + block_ids[None, :] * counts[:, None] // blocks + shifts
    span = jnp.clip(span, 0, seq_rows - lengths)
    before = own - jnp.concatenate([counts[:1], counts[:-1]])
    slot_rows = low + slot_of * capacity
    base_before = jnp.where(
        members == 0, low - own, jnp.concatenate([slot_rows[:1], slot_rows[:-1]]) - before
    )
    base_own = slot_rows - own
    base_after = (
        jnp.where(
            members == g - 1,
            low + g * capacity,
            jnp.concatenate([slot_rows[1:], slot_rows[-1:]]),
        )
        - after
    )
    is_before = span < own[:, None]
    is_own = span < after[:, None]
    first_base = jnp.where(
        is_before, base_before[:, None], jnp.where(is_own, base_own[:, None], base_after[:, None])
    )
    second_base = jnp.where(is_before, base_own[:, None], base_after[:, None])
    cut = jnp.where(
        is_before, own[:, None] - span, jnp.where(is_own, after[:, None] - span, block_size)
    )
    cut = jnp.minimum(cut, block_size)
    last_start = low + g * capacity + high
    first_start = jnp.clip(span + first_base, 0, last_start)
    second_start = jnp.clip(span + second_base, 0, last_start)
    info = jnp.stack(
        [first_start, second_start, cut, lengths]
    ).reshape(-1).astype(jnp.int32)

    flat = scales.reshape(-1)
    previous = jnp.maximum(q * g - 1, 0)
    pieces = [
        lax.dynamic_slice(
            flat, (previous * capacity + jnp.take(teacher_counts, previous) - low,), (low,)
        )
    ]
    for e in range(g):
        pieces.append(
            lax.dynamic_slice(flat, ((q * g + partner(p, e, g)[0]) * capacity,), (capacity,))
        )
    pieces.append(
        lax.dynamic_slice(flat, (jnp.minimum(q * g + g, n - 1) * capacity,), (high,))
    )
    row_scales = jnp.concatenate(pieces)
    tiles = -(-(last_start + 2 * block_size) // block_size)
    row_scales = jnp.pad(row_scales, (0, tiles * block_size - row_scales.shape[0]))
    row_scales = row_scales.reshape(tiles, 1, block_size)
    weights = weights.reshape(g * blocks, block_size, block_size)
    mixed = mix(g, blocks, info, row_scales, mapped, below, above, weights)
    row_grad, gain_grad = finish(
        g, n, tp, mixed.reshape(g, rows_here, nl * width), student_rows, student_gain[None, :], width
    )
    return (row_grad, gain_grad.reshape(-1))


def solution(mesh):
    placed = (
        P("seq", "tp"),
        P("tp"),
        P(),
        P("tp", "seq"),
        P("seq", "tp"),
        P("tp"),
        P("seq"),
        P("seq"),
        P("seq", None),
    )
    return jax.shard_map(
        shards, mesh=mesh, in_specs=placed, out_specs=(P("seq", "tp"), P("tp")), check_vma=False
    )
```

```python
import functools

import jax
import jax.numpy as jnp
from jax import lax
from jax.experimental import pallas as pl
from jax.experimental.pallas import tpu as pltpu
from jax.sharding import PartitionSpec as P

epsilon = 1e-06
MESH = pl.DeviceIdType.MESH
VMEM_LIMIT = 52 * 1024 * 1024


def group_size(count):
    size = 1
    while size * size < count:
        size *= 2
    return size


def partner(p, e, g):
    if g == 4:
        if e == 0:
            return p, p
        low, high = 1 - 2 * (p % 2), 2 - 4 * (p // 2)
        other = p + (low if e % 2 else 0) + (high if e // 2 else 0)
        return other, other
    return (p - e + g) % g, (p + e) % g


def gather_kernel(
    g, nq, tp, nh, np_,
    x_hbm, p_hbm, w_hbm, a_hbm,
    mapped, w_all, a_sum,
    xs, ps, part, recv, a_all, a_in,
    x_send, x_recv, u_send, d_send, p_recv, s_send, s_recv, a_send, a_recv, b_send, b_recv, t_send, t_recv, local,
):
    me, t = lax.axis_index("seq"), lax.axis_index("tp")
    p, q = me % g, me // g
    base = q * g
    half = xs.shape[1]
    nl = nq // tp

    barrier = pltpu.get_barrier_semaphore()
    n = g * nq
    for o in range(1, n):
        pl.semaphore_signal(barrier, inc=1, device_id=((me + o) % n, t), device_id_type=MESH)
    for o in range(1, tp):
        pl.semaphore_signal(barrier, inc=1, device_id=(me, (t + o) % tp), device_id_type=MESH)
    pl.semaphore_wait(barrier, n - 1 + tp - 1)

    def x_copy(source, e, h, member):
        return pltpu.make_async_remote_copy(
            src_ref=source, dst_ref=xs.at[e * nh + h],
            send_sem=x_send.at[e * nh + h], recv_sem=x_recv.at[e * nh + h],
            device_id=(base + member, t), device_id_type=MESH,
        )

    def own(h):
        return x_hbm.at[pl.ds(h * half, half)]

    piece = p_hbm.shape[0] // np_

    def p_copy(source, block, k, sem, seq):
        return pltpu.make_async_remote_copy(
            src_ref=source, dst_ref=ps.at[block, pl.ds(k * piece, piece)],
            send_sem=sem, recv_sem=p_recv.at[block * np_ + k],
            device_id=(seq, t), device_id_type=MESH,
        )

    relayed = g == 4
    direct = [1, 2] if relayed else list(range(1, g))

    def held(s, block, k):
        here = pl.ds(k * piece, piece)
        return p_hbm.at[here] if s == 0 else ps.at[block, here]

    def up(s, k):
        return p_copy(held(s, q - s, k), q - s, k, u_send.at[s * np_ + k], me + g)

    def down(s, k):
        return p_copy(held(s, q + s, k), q + s, k, d_send.at[s * np_ + k], me - g)

    def forward(s, k):
        @pl.when(q - s >= 0)
        def _():
            if s > 0:
                p_copy(held(0, q, k), q - s, k, u_send.at[0], me).wait_recv()

            @pl.when(q < nq - 1)
            def _():
                up(s, k).start()

        @pl.when(q + s < nq)
        def _():
            if s > 0:
                p_copy(held(0, q, k), q + s, k, u_send.at[0], me).wait_recv()

            @pl.when(q > 0)
            def _():
                down(s, k).start()

    first = []
    for h in range(nh):
        for e in direct:
            k = nh - 1 - h if e == 2 else h
            first.append((e, k))
    for e, h in first[: len(direct)]:
        x_copy(own(h), e, h, partner(p, e, g)[1]).start()
    for k in range(np_):
        forward(0, k)
    for e, h in first[len(direct):]:
        x_copy(own(h), e, h, partner(p, e, g)[1]).start()

    smalls = []
    for o in range(1, n):
        copy = pltpu.make_async_remote_copy(
            src_ref=a_hbm, dst_ref=a_all.at[me], send_sem=a_send.at[o], recv_sem=a_recv.at[o],
            device_id=((me + o) % n, t), device_id_type=MESH,
        )
        copy.start()
        smalls.append(copy)
    for e in range(1, g):
        copy = pltpu.make_async_remote_copy(
            src_ref=w_hbm, dst_ref=w_all.at[p], send_sem=s_send.at[e], recv_sem=s_recv.at[e],
            device_id=(base + (p + e) % g, t), device_id_type=MESH,
        )
        copy.start()
        smalls.append(copy)
    locals_ = [
        pltpu.make_async_copy(p_hbm, ps.at[q], local.at[0]),
        pltpu.make_async_copy(w_hbm, w_all.at[p], local.at[1]),
        pltpu.make_async_copy(a_hbm, a_all.at[me], local.at[2]),
    ]
    for h in range(nh):
        locals_.append(pltpu.make_async_copy(own(h), xs.at[h], local.at[3 + h]))
    for copy in locals_:
        copy.start()
    for copy in locals_:
        copy.wait()

    def a_copy(o):
        return pltpu.make_async_remote_copy(
            src_ref=a_all, dst_ref=a_in.at[o - 1],
            send_sem=b_send.at[o - 1], recv_sem=b_recv.at[o - 1],
            device_id=(me, (t + o) % tp), device_id_type=MESH,
        )

    def multiply(c0, c1, b0, b1):
        def blocks(b, carry):
            def chunks(c, inner):
                part[b, c] = jnp.dot(
                    xs[c], ps[b], preferred_element_type=jnp.float32
                ).astype(jnp.bfloat16)
                return inner

            return lax.fori_loop(c0, c1, chunks, carry)

        lax.fori_loop(b0, b1, blocks, 0)

    def near(s):
        return jnp.maximum(q - s, 0), jnp.minimum(q + s, nq - 1) + 1

    def at_distance(s, c0, c1):
        @pl.when(q - s >= 0)
        def _():
            multiply(c0, c1, q - s, q - s + 1)

        @pl.when(q + s < nq)
        def _():
            multiply(c0, c1, q + s, q + s + 1)

    forward(1, 0)
    for e, h in first[: len(direct)]:
        x_copy(own(h), e, h, partner(p, e, g)[1]).wait_recv()
        if relayed:
            x_copy(xs.at[e * nh + h], 3, h, partner(p, 3 - e, g)[1]).start()
    for k in range(1, np_):
        forward(1, k)
    far = nq - 1
    for s in range(2, far):
        forward(s, 0)
    for e, h in first[len(direct):]:
        x_copy(own(h), e, h, partner(p, e, g)[1]).wait_recv()
    for s in range(2, far):
        for k in range(1, np_):
            forward(s, k)
    early = (1 + len(direct)) * nh
    ranges = [(0, early), (early, g * nh)] if relayed else [(0, g * nh)]
    nr = len(ranges)

    def sum_copy(o, j, i):
        other = (t + o) % tp
        chunks = pl.ds(ranges[i][0], ranges[i][1] - ranges[i][0])
        sem = ((o - 1) * nl + j) * 2 + i
        return pltpu.make_async_remote_copy(
            src_ref=part.at[other * nl + j, chunks], dst_ref=recv.at[o - 1, j, chunks],
            send_sem=t_send.at[sem], recv_sem=t_recv.at[sem],
            device_id=(me, other), device_id_type=MESH,
        )

    def is_far(o, j):
        distance = (t + o) % tp * nl + j - q
        return (distance == far) | (distance == -far)

    sums = [(o, j) for o in range(1, tp) for j in range(nl)]
    for i in range(nr):
        if i == 1:
            for h in range(nh):
                x_copy(xs.at[3 * nh + h], 3, h, p).wait_recv()
        multiply(*ranges[i], *near(far - 1))
        for o, j in sums:
            @pl.when(jnp.logical_not(is_far(o, j)))
            def _():
                sum_copy(o, j, i).start()

        if i == 0:
            for copy in smalls:
                copy.wait_recv()
            for o in range(1, tp):
                a_copy(o).start()

    for k in range(np_):
        forward(far, k)
    at_distance(far, 0, g * nh)
    for o, j in sums:
        @pl.when(is_far(o, j))
        def _():
            for i in range(nr):
                sum_copy(o, j, i).start()

    total = a_all[...]
    for o in range(1, tp):
        a_copy(o).wait_recv()
        total += a_in[o - 1]
    a_sum[...] = total
    for o, j in sums:
        for i in range(nr):
            sum_copy(o, j, i).wait_recv()

    def add(i, carry):
        block, chunk = i // (g * nh), i % (g * nh)
        total = part[t * nl + block, chunk].astype(jnp.float32)
        for o in range(1, tp):
            total += recv[o - 1, block, chunk].astype(jnp.float32)
        mapped[block, chunk] = total.astype(jnp.bfloat16)
        return carry

    lax.fori_loop(0, nl * g * nh, add, 0)

    for copy in smalls:
        copy.wait_send()
    for o in range(1, tp):
        a_copy(o).wait_send()
    for o, j in sums:
        for i in range(nr):
            sum_copy(o, j, i).wait_send()
    for e, h in first:
        x_copy(own(h), e, h, partner(p, e, g)[1]).wait_send()
    if relayed:
        for e, h in first[: len(direct)]:
            x_copy(xs.at[e * nh + h], 3, h, partner(p, 3 - e, g)[1]).wait_send()
    for s in range(nq - 1):
        @pl.when((q - s >= 0) & (q < nq - 1))
        def _():
            for k in range(np_):
                up(s, k).wait_send()

        @pl.when((q + s < nq) & (q > 0))
        def _():
            for k in range(np_):
                down(s, k).wait_send()


def gather_map(g, nq, tp, x, p, w, a):
    rows, depth = x.shape
    width = p.shape[1]
    nh = 2 if rows % 32 == 0 else 1
    half = rows // nh
    np_ = 2
    nl = nq // tp
    any_spec = pl.BlockSpec(memory_space=pl.ANY)
    vmem = pl.BlockSpec(memory_space=pltpu.VMEM)
    dma = pltpu.SemaphoreType.DMA
    return pl.pallas_call(
        functools.partial(gather_kernel, g, nq, tp, nh, np_),
        out_shape=(
            jax.ShapeDtypeStruct((nl, g * nh, half, width), jnp.bfloat16),
            jax.ShapeDtypeStruct((g,) + w.shape, w.dtype),
            jax.ShapeDtypeStruct((g * nq,) + a.shape, a.dtype),
        ),
        in_specs=[any_spec] * 4,
        out_specs=(vmem, vmem, vmem),
        scratch_shapes=[
            pltpu.VMEM((g * nh, half, depth), jnp.bfloat16),
            pltpu.VMEM((nq, depth, width), jnp.bfloat16),
            pltpu.VMEM((nq, g * nh, half, width), jnp.bfloat16),
            pltpu.VMEM((max(tp - 1, 1), nl, g * nh, half, width), jnp.bfloat16),
            pltpu.VMEM((g * nq,) + a.shape, a.dtype),
            pltpu.VMEM((max(tp - 1, 1), g * nq) + a.shape, a.dtype),
            dma((g * nh,)),
            dma((g * nh,)),
            dma((nq * np_,)),
            dma((nq * np_,)),
            dma((nq * np_,)),
            dma((g,)),
            dma((g,)),
            dma((g * nq,)),
            dma((g * nq,)),
            dma((tp,)),
            dma((tp,)),
            dma((2 * tp * nl,)),
            dma((2 * tp * nl,)),
            dma((3 + nh,)),
        ],
        compiler_params=pltpu.CompilerParams(
            collective_id=0, has_side_effects=True, vmem_limit_bytes=VMEM_LIMIT
        ),
        cost_estimate=pl.CostEstimate(
            flops=2 * g * rows * depth * nq * width,
            bytes_accessed=2 * (g * rows * depth + nq * depth * width),
            transcendentals=0,
        ),
    )(x, p, w, a)


def mix_kernel(g, blocks, low, high, info, scales, mapped, below, above, weights, mixed, held):
    nl, width = mapped.shape[0], mapped.shape[2]
    size = weights.shape[1]
    live = low + mapped.shape[1] + high
    for z in range(nl):
        columns = slice(z * width, (z + 1) * width)
        held[0:low, columns] = below[z]
        held[low : live - high, columns] = mapped[z]
        held[live - high : live, columns] = above[z]
    held[live:, :] = jnp.zeros((held.shape[0] - live, held.shape[1]), held.dtype)
    lanes = lax.broadcasted_iota(jnp.int32, (size, size), 1)

    def one(b, carry):
        cut, length = info[2 * g * blocks + b], info[3 * g * blocks + b]
        source = jnp.where(lanes < length, weights[b].astype(jnp.float32), 0.0)
        total = None
        for part in range(2):
            start = info[part * g * blocks + b]
            kept = jnp.where((lanes < cut) if part == 0 else (lanes >= cut), source, 0.0)
            spread = jnp.concatenate([kept, jnp.zeros_like(kept)], axis=1)
            spread = pltpu.roll(spread, start % size, axis=1)
            tile = start // size
            scale = jnp.concatenate([scales[tile], scales[tile + 1]], axis=1)
            spread = (spread * scale).astype(jnp.bfloat16)
            rows = held[pl.ds(pl.multiple_of(tile * size, size), 2 * size), :]
            product = jnp.dot(spread, rows, preferred_element_type=jnp.float32)
            total = product if total is None else total + product
        mixed[b] = total.astype(jnp.bfloat16)
        return carry

    lax.fori_loop(0, g * blocks, one, 0)


def mix(g, blocks, info, scales, mapped, below, above, weights):
    nl, span_rows, width = mapped.shape
    low, high, size = below.shape[1], above.shape[1], weights.shape[1]
    vmem = pl.BlockSpec(memory_space=pltpu.VMEM)
    return pl.pallas_call(
        functools.partial(mix_kernel, g, blocks, low, high),
        out_shape=jax.ShapeDtypeStruct((g * blocks, size, nl * width), jnp.bfloat16),
        in_specs=[pl.BlockSpec(memory_space=pltpu.SMEM)] + [vmem] * 5,
        out_specs=vmem,
        scratch_shapes=[
            pltpu.VMEM((low + span_rows + high + 2 * size, nl * width), jnp.bfloat16)
        ],
        compiler_params=pltpu.CompilerParams(vmem_limit_bytes=VMEM_LIMIT),
    )(info, scales, mapped, below, above, weights)


def finish_kernel(
    g, n, tp, nl, width, student_width, step,
    mixed, student, gain, row_grad, gain_grad,
    target, sums, sums_in, terms, gained, gained_in,
    m_send, m_recv, t_send, t_recv, g_send, g_recv,
):
    me, t = lax.axis_index("seq"), lax.axis_index("tp")
    p = me % g
    base = me - p
    rows = student.shape[0]
    barrier = pltpu.get_barrier_semaphore()
    for o in range(1, n):
        pl.semaphore_signal(barrier, inc=1, device_id=((me + o) % n, t), device_id_type=MESH)
    for o in range(1, tp):
        pl.semaphore_signal(barrier, inc=1, device_id=(me, (t + o) % tp), device_id_type=MESH)
    pl.semaphore_wait(barrier, n - 1 + tp - 1)

    copies = []
    for e in range(1, g):
        member = partner(p, e, g)[1]
        copy = pltpu.make_async_remote_copy(
            src_ref=mixed.at[member], dst_ref=target.at[p],
            send_sem=m_send.at[e], recv_sem=m_recv.at[e],
            device_id=(base + member, t), device_id_type=MESH,
        )
        copy.start()
        copies.append(copy)
    own = pltpu.make_async_copy(mixed.at[p], target.at[p], m_send.at[0])
    own.start()
    own.wait()
    for copy in copies:
        copy.wait_recv()

    tiles = [(m, z) for z in range(nl) for m in range(g)]

    def load(r, m, z):
        here = pl.ds(pl.multiple_of(r * step, step), step)
        start = (z * g + m) * width
        s = student[here, start : start + width].astype(jnp.float32)
        v = target[m, here, z * width : (z + 1) * width].astype(jnp.float32)
        return s, v, gain[:, start : start + width]

    lanes = lax.broadcasted_iota(jnp.int32, (step, 128), 1)

    def count(r, carry):
        parts = [0.0] * 4
        for m, z in tiles:
            s, v, gn = load(r, m, z)
            sg = s * gn
            for k, term in enumerate((s * s, sg * sg, v * v, sg * v)):
                parts[k] = parts[k] + term
        packed = jnp.zeros((step, 128), jnp.float32)
        for k in range(4):
            packed = jnp.where(lanes == k, jnp.sum(parts[k], axis=1, keepdims=True), packed)
        sums[pl.ds(pl.multiple_of(r * step, step), step), :] = packed
        return carry

    lax.fori_loop(0, rows // step, count, 0)

    pairs = []
    for o in range(1, tp):
        copy = pltpu.make_async_remote_copy(
            src_ref=sums, dst_ref=sums_in.at[o - 1],
            send_sem=t_send.at[o - 1], recv_sem=t_recv.at[o - 1],
            device_id=(me, (t + o) % tp), device_id_type=MESH,
        )
        copy.start()
        pairs.append(copy)
    for copy in pairs:
        copy.wait_recv()

    terms[...] = jnp.zeros_like(terms)

    def grade(r, carry):
        here = pl.ds(pl.multiple_of(r * step, step), step)
        total = sums[here, :]
        for o in range(1, tp):
            total += sums_in[o - 1, here, :]
        ss, gg, vv, sv = [total[:, k : k + 1] for k in range(4)]
        s_scale = lax.rsqrt(ss / student_width + epsilon)
        v_scale = lax.rsqrt(vv / student_width + epsilon)
        inner = (s_scale * s_scale * gg - s_scale * v_scale * sv) / student_width
        for m, z in tiles:
            s, v, gn = load(r, m, z)
            start = (z * g + m) * width
            hat = s * s_scale
            residual = hat * gn - v * v_scale
            out = s_scale * (residual * gn - hat * inner)
            row_grad[here, start : start + width] = out.astype(row_grad.dtype)
            product = residual * hat
            terms[:, start : start + width] += sum(
                product[8 * i : 8 * i + 8] for i in range(step // 8)
            )
        return carry

    lax.fori_loop(0, rows // step, grade, 0)

    gained[...] = jnp.sum(terms[...], axis=0, keepdims=True)
    lasts = []
    for o in range(1, n):
        copy = pltpu.make_async_remote_copy(
            src_ref=gained, dst_ref=gained_in.at[o],
            send_sem=g_send.at[o], recv_sem=g_recv.at[o],
            device_id=((me + o) % n, t), device_id_type=MESH,
        )
        copy.start()
        lasts.append(copy)
    total = gained[...]
    for o, copy in zip(range(1, n), lasts):
        copy.wait_recv()
        total += gained_in[o]
    gain_grad[...] = total / (rows * n)
    for copy in copies + pairs + lasts:
        copy.wait_send()


def finish(g, n, tp, mixed, student, gain, width):
    rows, columns = student.shape
    nl = mixed.shape[2] // width
    vmem = pl.BlockSpec(memory_space=pltpu.VMEM)
    dma = pltpu.SemaphoreType.DMA
    step = 32 if rows % 32 == 0 else 16
    return pl.pallas_call(
        functools.partial(finish_kernel, g, n, tp, nl, width, columns * tp, step),
        out_shape=(
            jax.ShapeDtypeStruct((rows, columns), jnp.bfloat16),
            jax.ShapeDtypeStruct((1, columns), jnp.float32),
        ),
        in_specs=[vmem] * 3,
        out_specs=(vmem, vmem),
        scratch_shapes=[
            pltpu.VMEM(mixed.shape, mixed.dtype),
            pltpu.VMEM((rows, 128), jnp.float32),
            pltpu.VMEM((max(tp - 1, 1), rows, 128), jnp.float32),
            pltpu.VMEM((8, columns), jnp.float32),
            pltpu.VMEM((1, columns), jnp.float32),
            pltpu.VMEM((n, 1, columns), jnp.float32),
            dma((g,)),
            dma((g,)),
            dma((tp,)),
            dma((tp,)),
            dma((n,)),
            dma((n,)),
        ],
        compiler_params=pltpu.CompilerParams(
            collective_id=1, has_side_effects=True, vmem_limit_bytes=VMEM_LIMIT
        ),
    )(mixed, student, gain)


def shards(
    teacher_rows,
    teacher_gain,
    teacher_counts,
    projector,
    student_rows,
    student_gain,
    span_shift,
    span_len,
    align_weights,
):
    n, tp = lax.axis_size("seq"), lax.axis_size("tp")
    me = lax.axis_index("seq")
    g = group_size(n)
    nq = n // g
    p, q = me % g, me // g
    teacher_width = teacher_rows.shape[1] * tp
    student_width = student_rows.shape[1] * tp
    capacity = teacher_rows.shape[0]
    rows_here = student_rows.shape[0]
    block_size = align_weights.shape[1]
    blocks = span_shift.shape[0]
    width = projector.shape[1]
    nl = nq // tp
    seq_rows = rows_here * n

    teacher_float = teacher_rows.astype(jnp.float32)
    squares = jnp.sum(teacher_float * teacher_float, axis=1)
    aux = jnp.concatenate(
        [squares, span_shift.astype(jnp.float32), span_len.astype(jnp.float32)]
    )
    aux_rows = -(-aux.shape[0] // 1024) * 8
    aux = jnp.pad(aux, (0, aux_rows * 128 - aux.shape[0])).reshape(aux_rows, 128)
    scaled = (projector.astype(jnp.float32) * teacher_gain[:, None]).astype(jnp.bfloat16)
    mapped, weights, aux_all = gather_map(g, nq, tp, teacher_rows, scaled, align_weights, aux)
    aux_all = aux_all.reshape(n, aux_rows * 128)
    square_sums = aux_all[:, :capacity]
    scales = lax.rsqrt(square_sums / teacher_width + epsilon)
    spans = lax.dynamic_slice(aux_all, (q * g, capacity), (g, 2 * blocks))
    spans = jnp.round(spans / tp).astype(jnp.int32)
    shifts, lengths = spans[:, :blocks], spans[:, blocks:]

    members = jnp.arange(g, dtype=jnp.int32)
    if g == 4:
        slot_of = jnp.bitwise_xor(members, p)
    else:
        slot_of = (p - members + g) % g
    mapped = mapped.reshape(nl, g * capacity, width)

    starts = jnp.cumsum(teacher_counts) - teacher_counts
    low = block_size
    high = 2 * block_size - (2 * rows_here - capacity) // blocks
    last_count = jnp.take(teacher_counts, q * g + g - 1)
    tail_at = slot_of[g - 1] * capacity + last_count - low
    tail = lax.dynamic_slice(mapped, (0, tail_at, 0), (nl, low, width))
    head = lax.dynamic_slice(mapped, (0, slot_of[0] * capacity, 0), (nl, high, width))
    below = lax.ppermute(tail, "seq", [(i, i + g) for i in range(n - g)])
    above = lax.ppermute(head, "seq", [(i + g, i) for i in range(n - g)])

    ids = q * g + members
    counts = lax.dynamic_slice(teacher_counts, (q * g,), (g,))
    own = lax.dynamic_slice(starts, (q * g,), (g,))
    after = own + counts
    block_ids = jnp.arange(blocks, dtype=jnp.int32)
    span = own[:, None] + block_ids[None, :] * counts[:, None] // blocks + shifts
    span = jnp.clip(span, 0, seq_rows - lengths)
    before = own - jnp.concatenate([counts[:1], counts[:-1]])
    slot_rows = low + slot_of * capacity
    base_before = jnp.where(
        members == 0, low - own, jnp.concatenate([slot_rows[:1], slot_rows[:-1]]) - before
    )
    base_own = slot_rows - own
    base_after = (
        jnp.where(
            members == g - 1,
            low + g * capacity,
            jnp.concatenate([slot_rows[1:], slot_rows[-1:]]),
        )
        - after
    )
    is_before = span < own[:, None]
    is_own = span < after[:, None]
    first_base = jnp.where(
        is_before, base_before[:, None], jnp.where(is_own, base_own[:, None], base_after[:, None])
    )
    second_base = jnp.where(is_before, base_own[:, None], base_after[:, None])
    cut = jnp.where(
        is_before, own[:, None] - span, jnp.where(is_own, after[:, None] - span, block_size)
    )
    cut = jnp.minimum(cut, block_size)
    last_start = low + g * capacity + high
    first_start = jnp.clip(span + first_base, 0, last_start)
    second_start = jnp.clip(span + second_base, 0, last_start)
    info = jnp.stack(
        [first_start, second_start, cut, lengths]
    ).reshape(-1).astype(jnp.int32)

    flat = scales.reshape(-1)
    previous = jnp.maximum(q * g - 1, 0)
    pieces = [
        lax.dynamic_slice(
            flat, (previous * capacity + jnp.take(teacher_counts, previous) - low,), (low,)
        )
    ]
    for e in range(g):
        pieces.append(
            lax.dynamic_slice(flat, ((q * g + partner(p, e, g)[0]) * capacity,), (capacity,))
        )
    pieces.append(
        lax.dynamic_slice(flat, (jnp.minimum(q * g + g, n - 1) * capacity,), (high,))
    )
    row_scales = jnp.concatenate(pieces)
    tiles = -(-(last_start + 2 * block_size) // block_size)
    row_scales = jnp.pad(row_scales, (0, tiles * block_size - row_scales.shape[0]))
    row_scales = row_scales.reshape(tiles, 1, block_size)
    weights = weights.reshape(g * blocks, block_size, block_size)
    mixed = mix(g, blocks, info, row_scales, mapped, below, above, weights)
    row_grad, gain_grad = finish(
        g, n, tp, mixed.reshape(g, rows_here, nl * width), student_rows, student_gain[None, :], width
    )
    return (row_grad, gain_grad.reshape(-1))


def solution(mesh):
    placed = (
        P("seq", "tp"),
        P("tp"),
        P(),
        P("tp", "seq"),
        P("seq", "tp"),
        P("tp"),
        P("seq"),
        P("seq"),
        P("seq", None),
    )
    return jax.shard_map(
        shards, mesh=mesh, in_specs=placed, out_specs=(P("seq", "tp"), P("tp")), check_vma=False
    )
```

```python
import functools

import jax
import jax.numpy as jnp
from jax import lax
from jax.experimental import pallas as pl
from jax.experimental.pallas import tpu as pltpu
from jax.sharding import PartitionSpec as P

epsilon = 1e-06
MESH = pl.DeviceIdType.MESH
VMEM_LIMIT = 52 * 1024 * 1024


def group_size(count):
    size = 1
    while size * size < count:
        size *= 2
    return size


def partner(p, e, g):
    if g == 4:
        if e == 0:
            return p, p
        low, high = 1 - 2 * (p % 2), 2 - 4 * (p // 2)
        other = p + (low if e % 2 else 0) + (high if e // 2 else 0)
        return other, other
    return (p - e + g) % g, (p + e) % g


def gather_kernel(
    g, nq, tp, nh, np_,
    x_hbm, p_hbm, w_hbm, a_hbm,
    mapped, w_all, a_sum,
    xs, ps, part, recv, acc, a_all, a_in,
    x_send, x_recv, u_send, d_send, p_recv, s_send, s_recv, a_send, a_recv, b_send, b_recv, t_send, t_recv, local,
):
    me, t = lax.axis_index("seq"), lax.axis_index("tp")
    p, q = me % g, me // g
    base = q * g
    half = xs.shape[1]
    nl = nq // tp

    barrier = pltpu.get_barrier_semaphore()
    n = g * nq
    for o in range(1, n):
        pl.semaphore_signal(barrier, inc=1, device_id=((me + o) % n, t), device_id_type=MESH)
    for o in range(1, tp):
        pl.semaphore_signal(barrier, inc=1, device_id=(me, (t + o) % tp), device_id_type=MESH)
    pl.semaphore_wait(barrier, n - 1 + tp - 1)

    def x_copy(source, e, h, member):
        return pltpu.make_async_remote_copy(
            src_ref=source, dst_ref=xs.at[e * nh + h],
            send_sem=x_send.at[e * nh + h], recv_sem=x_recv.at[e * nh + h],
            device_id=(base + member, t), device_id_type=MESH,
        )

    def own(h):
        return x_hbm.at[pl.ds(h * half, half)]

    piece = p_hbm.shape[0] // np_

    def p_copy(source, block, k, sem, seq):
        return pltpu.make_async_remote_copy(
            src_ref=source, dst_ref=ps.at[block, pl.ds(k * piece, piece)],
            send_sem=sem, recv_sem=p_recv.at[block * np_ + k],
            device_id=(seq, t), device_id_type=MESH,
        )

    relayed = g == 4
    direct = [1, 2] if relayed else list(range(1, g))

    def held(s, block, k):
        here = pl.ds(k * piece, piece)
        return p_hbm.at[here] if s == 0 else ps.at[block, here]

    def up(s, k):
        return p_copy(held(s, q - s, k), q - s, k, u_send.at[s * np_ + k], me + g)

    def down(s, k):
        return p_copy(held(s, q + s, k), q + s, k, d_send.at[s * np_ + k], me - g)

    def forward(s, k):
        @pl.when(q - s >= 0)
        def _():
            if s > 0:
                p_copy(held(0, q, k), q - s, k, u_send.at[0], me).wait_recv()

            @pl.when(q < nq - 1)
            def _():
                up(s, k).start()

        @pl.when(q + s < nq)
        def _():
            if s > 0:
                p_copy(held(0, q, k), q + s, k, u_send.at[0], me).wait_recv()

            @pl.when(q > 0)
            def _():
                down(s, k).start()

    first = []
    for h in range(nh):
        for e in direct:
            k = nh - 1 - h if e == 2 else h
            first.append((e, k))
    for e, h in first[: len(direct)]:
        x_copy(own(h), e, h, partner(p, e, g)[1]).start()
    for k in range(np_):
        forward(0, k)
    for e, h in first[len(direct):]:
        x_copy(own(h), e, h, partner(p, e, g)[1]).start()

    smalls = []
    for o in range(1, n):
        copy = pltpu.make_async_remote_copy(
            src_ref=a_hbm, dst_ref=a_all.at[me], send_sem=a_send.at[o], recv_sem=a_recv.at[o],
            device_id=((me + o) % n, t), device_id_type=MESH,
        )
        copy.start()
        smalls.append(copy)
    for e in range(1, g):
        copy = pltpu.make_async_remote_copy(
            src_ref=w_hbm, dst_ref=w_all.at[p], send_sem=s_send.at[e], recv_sem=s_recv.at[e],
            device_id=(base + (p + e) % g, t), device_id_type=MESH,
        )
        copy.start()
        smalls.append(copy)
    locals_ = [
        pltpu.make_async_copy(p_hbm, ps.at[q], local.at[0]),
        pltpu.make_async_copy(w_hbm, w_all.at[p], local.at[1]),
        pltpu.make_async_copy(a_hbm, a_all.at[me], local.at[2]),
    ]
    for h in range(nh):
        locals_.append(pltpu.make_async_copy(own(h), xs.at[h], local.at[3 + h]))
    for copy in locals_:
        copy.start()
    for copy in locals_:
        copy.wait()

    def a_copy(o):
        return pltpu.make_async_remote_copy(
            src_ref=a_all, dst_ref=a_in.at[o - 1],
            send_sem=b_send.at[o - 1], recv_sem=b_recv.at[o - 1],
            device_id=(me, (t + o) % tp), device_id_type=MESH,
        )

    def multiply(c0, c1, b0, b1):
        def blocks(b, carry):
            def chunks(c, inner):
                part[b, c] = jnp.dot(
                    xs[c], ps[b], preferred_element_type=jnp.float32
                ).astype(jnp.bfloat16)
                return inner

            return lax.fori_loop(c0, c1, chunks, carry)

        lax.fori_loop(b0, b1, blocks, 0)

    def near(s):
        return jnp.maximum(q - s, 0), jnp.minimum(q + s, nq - 1) + 1

    forward(1, 0)
    for e, h in first[: len(direct)]:
        x_copy(own(h), e, h, partner(p, e, g)[1]).wait_recv()
        if relayed:
            x_copy(xs.at[e * nh + h], 3, h, partner(p, 3 - e, g)[1]).start()
    for k in range(1, np_):
        forward(1, k)
    far = nq - 1
    for s in range(2, far):
        forward(s, 0)
    for e, h in first[len(direct):]:
        x_copy(own(h), e, h, partner(p, e, g)[1]).wait_recv()
    for s in range(2, far):
        for k in range(1, np_):
            forward(s, k)
    early = (1 + len(direct)) * nh
    ranges = [(0, early), (early, g * nh)] if relayed else [(0, g * nh)]
    nr = len(ranges)

    def sum_copy(o, j, i):
        other = (t + o) % tp
        chunks = pl.ds(ranges[i][0], ranges[i][1] - ranges[i][0])
        sem = ((o - 1) * nl + j) * 2 + i
        return pltpu.make_async_remote_copy(
            src_ref=part.at[other * nl + j, chunks], dst_ref=recv.at[o - 1, j, chunks],
            send_sem=t_send.at[sem], recv_sem=t_recv.at[sem],
            device_id=(me, other), device_id_type=MESH,
        )

    def is_far(o, j):
        distance = (t + o) % tp * nl + j - q
        return (distance == far) | (distance == -far)

    sums = [(o, j) for o in range(1, tp) for j in range(nl)]
    for i in range(nr):
        if i == 1:
            for h in range(nh):
                x_copy(xs.at[3 * nh + h], 3, h, p).wait_recv()
        multiply(*ranges[i], *near(far - 1))
        for o, j in sums:
            @pl.when(jnp.logical_not(is_far(o, j)))
            def _():
                sum_copy(o, j, i).start()

        if i == 0:
            for copy in smalls:
                copy.wait_recv()
            for o in range(1, tp):
                a_copy(o).start()

    def last(b, k):
        here = slice(k * piece, (k + 1) * piece)

        def chunks(c, carry):
            term = jnp.dot(xs[c, :, here], ps[b, here, :], preferred_element_type=jnp.float32)
            if k > 0:
                term += acc[c]
            if k < np_ - 1:
                acc[c] = term
            else:
                part[b, c] = term.astype(jnp.bfloat16)
            return carry

        lax.fori_loop(0, g * nh, chunks, 0)

    for k in range(np_):
        forward(far, k)

        @pl.when(q - far >= 0)
        def _():
            last(q - far, k)

        @pl.when(q + far < nq)
        def _():
            last(q + far, k)

    for o, j in sums:
        @pl.when(is_far(o, j))
        def _():
            for i in range(nr):
                sum_copy(o, j, i).start()

    total = a_all[...]
    for o in range(1, tp):
        a_copy(o).wait_recv()
        total += a_in[o - 1]
    a_sum[...] = total
    for o, j in sums:
        for i in range(nr):
            sum_copy(o, j, i).wait_recv()

    def add(i, carry):
        block, chunk = i // (g * nh), i % (g * nh)
        total = part[t * nl + block, chunk].astype(jnp.float32)
        for o in range(1, tp):
            total += recv[o - 1, block, chunk].astype(jnp.float32)
        mapped[block, chunk] = total.astype(jnp.bfloat16)
        return carry

    lax.fori_loop(0, nl * g * nh, add, 0)

    for copy in smalls:
        copy.wait_send()
    for o in range(1, tp):
        a_copy(o).wait_send()
    for o, j in sums:
        for i in range(nr):
            sum_copy(o, j, i).wait_send()
    for e, h in first:
        x_copy(own(h), e, h, partner(p, e, g)[1]).wait_send()
    if relayed:
        for e, h in first[: len(direct)]:
            x_copy(xs.at[e * nh + h], 3, h, partner(p, 3 - e, g)[1]).wait_send()
    for s in range(nq - 1):
        @pl.when((q - s >= 0) & (q < nq - 1))
        def _():
            for k in range(np_):
                up(s, k).wait_send()

        @pl.when((q + s < nq) & (q > 0))
        def _():
            for k in range(np_):
                down(s, k).wait_send()


def gather_map(g, nq, tp, x, p, w, a):
    rows, depth = x.shape
    width = p.shape[1]
    nh = 2 if rows % 32 == 0 else 1
    half = rows // nh
    np_ = 2
    nl = nq // tp
    any_spec = pl.BlockSpec(memory_space=pl.ANY)
    vmem = pl.BlockSpec(memory_space=pltpu.VMEM)
    dma = pltpu.SemaphoreType.DMA
    return pl.pallas_call(
        functools.partial(gather_kernel, g, nq, tp, nh, np_),
        out_shape=(
            jax.ShapeDtypeStruct((nl, g * nh, half, width), jnp.bfloat16),
            jax.ShapeDtypeStruct((g,) + w.shape, w.dtype),
            jax.ShapeDtypeStruct((g * nq,) + a.shape, a.dtype),
        ),
        in_specs=[any_spec] * 4,
        out_specs=(vmem, vmem, vmem),
        scratch_shapes=[
            pltpu.VMEM((g * nh, half, depth), jnp.bfloat16),
            pltpu.VMEM((nq, depth, width), jnp.bfloat16),
            pltpu.VMEM((nq, g * nh, half, width), jnp.bfloat16),
            pltpu.VMEM((max(tp - 1, 1), nl, g * nh, half, width), jnp.bfloat16),
            pltpu.VMEM((g * nh, half, width), jnp.float32),
            pltpu.VMEM((g * nq,) + a.shape, a.dtype),
            pltpu.VMEM((max(tp - 1, 1), g * nq) + a.shape, a.dtype),
            dma((g * nh,)),
            dma((g * nh,)),
            dma((nq * np_,)),
            dma((nq * np_,)),
            dma((nq * np_,)),
            dma((g,)),
            dma((g,)),
            dma((g * nq,)),
            dma((g * nq,)),
            dma((tp,)),
            dma((tp,)),
            dma((2 * tp * nl,)),
            dma((2 * tp * nl,)),
            dma((3 + nh,)),
        ],
        compiler_params=pltpu.CompilerParams(
            collective_id=0, has_side_effects=True, vmem_limit_bytes=VMEM_LIMIT
        ),
        cost_estimate=pl.CostEstimate(
            flops=2 * g * rows * depth * nq * width,
            bytes_accessed=2 * (g * rows * depth + nq * depth * width),
            transcendentals=0,
        ),
    )(x, p, w, a)


def mix_kernel(g, blocks, low, high, info, scales, mapped, below, above, weights, mixed, held):
    nl, width = mapped.shape[0], mapped.shape[2]
    size = weights.shape[1]
    live = low + mapped.shape[1] + high
    for z in range(nl):
        columns = slice(z * width, (z + 1) * width)
        held[0:low, columns] = below[z]
        held[low : live - high, columns] = mapped[z]
        held[live - high : live, columns] = above[z]
    held[live:, :] = jnp.zeros((held.shape[0] - live, held.shape[1]), held.dtype)
    lanes = lax.broadcasted_iota(jnp.int32, (size, size), 1)

    def one(b, carry):
        cut, length = info[2 * g * blocks + b], info[3 * g * blocks + b]
        source = jnp.where(lanes < length, weights[b].astype(jnp.float32), 0.0)
        total = None
        for part in range(2):
            start = info[part * g * blocks + b]
            kept = jnp.where((lanes < cut) if part == 0 else (lanes >= cut), source, 0.0)
            spread = jnp.concatenate([kept, jnp.zeros_like(kept)], axis=1)
            spread = pltpu.roll(spread, start % size, axis=1)
            tile = start // size
            scale = jnp.concatenate([scales[tile], scales[tile + 1]], axis=1)
            spread = (spread * scale).astype(jnp.bfloat16)
            rows = held[pl.ds(pl.multiple_of(tile * size, size), 2 * size), :]
            product = jnp.dot(spread, rows, preferred_element_type=jnp.float32)
            total = product if total is None else total + product
        mixed[b] = total.astype(jnp.bfloat16)
        return carry

    lax.fori_loop(0, g * blocks, one, 0)


def mix(g, blocks, info, scales, mapped, below, above, weights):
    nl, span_rows, width = mapped.shape
    low, high, size = below.shape[1], above.shape[1], weights.shape[1]
    vmem = pl.BlockSpec(memory_space=pltpu.VMEM)
    return pl.pallas_call(
        functools.partial(mix_kernel, g, blocks, low, high),
        out_shape=jax.ShapeDtypeStruct((g * blocks, size, nl * width), jnp.bfloat16),
        in_specs=[pl.BlockSpec(memory_space=pltpu.SMEM)] + [vmem] * 5,
        out_specs=vmem,
        scratch_shapes=[
            pltpu.VMEM((low + span_rows + high + 2 * size, nl * width), jnp.bfloat16)
        ],
        compiler_params=pltpu.CompilerParams(vmem_limit_bytes=VMEM_LIMIT),
    )(info, scales, mapped, below, above, weights)


def finish_kernel(
    g, n, tp, nl, width, student_width, step,
    mixed, student, gain, row_grad, gain_grad,
    target, sums, sums_in, terms, gained, gained_in,
    m_send, m_recv, t_send, t_recv, g_send, g_recv,
):
    me, t = lax.axis_index("seq"), lax.axis_index("tp")
    p = me % g
    base = me - p
    rows = student.shape[0]
    barrier = pltpu.get_barrier_semaphore()
    for o in range(1, n):
        pl.semaphore_signal(barrier, inc=1, device_id=((me + o) % n, t), device_id_type=MESH)
    for o in range(1, tp):
        pl.semaphore_signal(barrier, inc=1, device_id=(me, (t + o) % tp), device_id_type=MESH)
    pl.semaphore_wait(barrier, n - 1 + tp - 1)

    copies = []
    for e in range(1, g):
        member = partner(p, e, g)[1]
        copy = pltpu.make_async_remote_copy(
            src_ref=mixed.at[member], dst_ref=target.at[p],
            send_sem=m_send.at[e], recv_sem=m_recv.at[e],
            device_id=(base + member, t), device_id_type=MESH,
        )
        copy.start()
        copies.append(copy)
    own = pltpu.make_async_copy(mixed.at[p], target.at[p], m_send.at[0])
    own.start()
    own.wait()
    for copy in copies:
        copy.wait_recv()

    tiles = [(m, z) for z in range(nl) for m in range(g)]

    def load(r, m, z):
        here = pl.ds(pl.multiple_of(r * step, step), step)
        start = (z * g + m) * width
        s = student[here, start : start + width].astype(jnp.float32)
        v = target[m, here, z * width : (z + 1) * width].astype(jnp.float32)
        return s, v, gain[:, start : start + width]

    lanes = lax.broadcasted_iota(jnp.int32, (step, 128), 1)

    def count(r, carry):
        parts = [0.0] * 4
        for m, z in tiles:
            s, v, gn = load(r, m, z)
            sg = s * gn
            for k, term in enumerate((s * s, sg * sg, v * v, sg * v)):
                parts[k] = parts[k] + term
        packed = jnp.zeros((step, 128), jnp.float32)
        for k in range(4):
            packed = jnp.where(lanes == k, jnp.sum(parts[k], axis=1, keepdims=True), packed)
        sums[pl.ds(pl.multiple_of(r * step, step), step), :] = packed
        return carry

    lax.fori_loop(0, rows // step, count, 0)

    pairs = []
    for o in range(1, tp):
        copy = pltpu.make_async_remote_copy(
            src_ref=sums, dst_ref=sums_in.at[o - 1],
            send_sem=t_send.at[o - 1], recv_sem=t_recv.at[o - 1],
            device_id=(me, (t + o) % tp), device_id_type=MESH,
        )
        copy.start()
        pairs.append(copy)
    for copy in pairs:
        copy.wait_recv()

    terms[...] = jnp.zeros_like(terms)

    def grade(r, carry):
        here = pl.ds(pl.multiple_of(r * step, step), step)
        total = sums[here, :]
        for o in range(1, tp):
            total += sums_in[o - 1, here, :]
        ss, gg, vv, sv = [total[:, k : k + 1] for k in range(4)]
        s_scale = lax.rsqrt(ss / student_width + epsilon)
        v_scale = lax.rsqrt(vv / student_width + epsilon)
        inner = (s_scale * s_scale * gg - s_scale * v_scale * sv) / student_width
        for m, z in tiles:
            s, v, gn = load(r, m, z)
            start = (z * g + m) * width
            hat = s * s_scale
            residual = hat * gn - v * v_scale
            out = s_scale * (residual * gn - hat * inner)
            row_grad[here, start : start + width] = out.astype(row_grad.dtype)
            product = residual * hat
            terms[:, start : start + width] += sum(
                product[8 * i : 8 * i + 8] for i in range(step // 8)
            )
        return carry

    lax.fori_loop(0, rows // step, grade, 0)

    gained[...] = jnp.sum(terms[...], axis=0, keepdims=True)
    lasts = []
    for o in range(1, n):
        copy = pltpu.make_async_remote_copy(
            src_ref=gained, dst_ref=gained_in.at[o],
            send_sem=g_send.at[o], recv_sem=g_recv.at[o],
            device_id=((me + o) % n, t), device_id_type=MESH,
        )
        copy.start()
        lasts.append(copy)
    total = gained[...]
    for o, copy in zip(range(1, n), lasts):
        copy.wait_recv()
        total += gained_in[o]
    gain_grad[...] = total / (rows * n)
    for copy in copies + pairs + lasts:
        copy.wait_send()


def finish(g, n, tp, mixed, student, gain, width):
    rows, columns = student.shape
    nl = mixed.shape[2] // width
    vmem = pl.BlockSpec(memory_space=pltpu.VMEM)
    dma = pltpu.SemaphoreType.DMA
    step = 32 if rows % 32 == 0 else 16
    return pl.pallas_call(
        functools.partial(finish_kernel, g, n, tp, nl, width, columns * tp, step),
        out_shape=(
            jax.ShapeDtypeStruct((rows, columns), jnp.bfloat16),
            jax.ShapeDtypeStruct((1, columns), jnp.float32),
        ),
        in_specs=[vmem] * 3,
        out_specs=(vmem, vmem),
        scratch_shapes=[
            pltpu.VMEM(mixed.shape, mixed.dtype),
            pltpu.VMEM((rows, 128), jnp.float32),
            pltpu.VMEM((max(tp - 1, 1), rows, 128), jnp.float32),
            pltpu.VMEM((8, columns), jnp.float32),
            pltpu.VMEM((1, columns), jnp.float32),
            pltpu.VMEM((n, 1, columns), jnp.float32),
            dma((g,)),
            dma((g,)),
            dma((tp,)),
            dma((tp,)),
            dma((n,)),
            dma((n,)),
        ],
        compiler_params=pltpu.CompilerParams(
            collective_id=1, has_side_effects=True, vmem_limit_bytes=VMEM_LIMIT
        ),
    )(mixed, student, gain)


def shards(
    teacher_rows,
    teacher_gain,
    teacher_counts,
    projector,
    student_rows,
    student_gain,
    span_shift,
    span_len,
    align_weights,
):
    n, tp = lax.axis_size("seq"), lax.axis_size("tp")
    me = lax.axis_index("seq")
    g = group_size(n)
    nq = n // g
    p, q = me % g, me // g
    teacher_width = teacher_rows.shape[1] * tp
    student_width = student_rows.shape[1] * tp
    capacity = teacher_rows.shape[0]
    rows_here = student_rows.shape[0]
    block_size = align_weights.shape[1]
    blocks = span_shift.shape[0]
    width = projector.shape[1]
    nl = nq // tp
    seq_rows = rows_here * n

    teacher_float = teacher_rows.astype(jnp.float32)
    squares = jnp.sum(teacher_float * teacher_float, axis=1)
    aux = jnp.concatenate(
        [squares, span_shift.astype(jnp.float32), span_len.astype(jnp.float32)]
    )
    aux_rows = -(-aux.shape[0] // 1024) * 8
    aux = jnp.pad(aux, (0, aux_rows * 128 - aux.shape[0])).reshape(aux_rows, 128)
    scaled = (projector.astype(jnp.float32) * teacher_gain[:, None]).astype(jnp.bfloat16)
    mapped, weights, aux_all = gather_map(g, nq, tp, teacher_rows, scaled, align_weights, aux)
    aux_all = aux_all.reshape(n, aux_rows * 128)
    square_sums = aux_all[:, :capacity]
    scales = lax.rsqrt(square_sums / teacher_width + epsilon)
    spans = lax.dynamic_slice(aux_all, (q * g, capacity), (g, 2 * blocks))
    spans = jnp.round(spans / tp).astype(jnp.int32)
    shifts, lengths = spans[:, :blocks], spans[:, blocks:]

    members = jnp.arange(g, dtype=jnp.int32)
    if g == 4:
        slot_of = jnp.bitwise_xor(members, p)
    else:
        slot_of = (p - members + g) % g
    mapped = mapped.reshape(nl, g * capacity, width)

    starts = jnp.cumsum(teacher_counts) - teacher_counts
    low = block_size
    high = 2 * block_size - (2 * rows_here - capacity) // blocks
    last_count = jnp.take(teacher_counts, q * g + g - 1)
    tail_at = slot_of[g - 1] * capacity + last_count - low
    tail = lax.dynamic_slice(mapped, (0, tail_at, 0), (nl, low, width))
    head = lax.dynamic_slice(mapped, (0, slot_of[0] * capacity, 0), (nl, high, width))
    below = lax.ppermute(tail, "seq", [(i, i + g) for i in range(n - g)])
    above = lax.ppermute(head, "seq", [(i + g, i) for i in range(n - g)])

    ids = q * g + members
    counts = lax.dynamic_slice(teacher_counts, (q * g,), (g,))
    own = lax.dynamic_slice(starts, (q * g,), (g,))
    after = own + counts
    block_ids = jnp.arange(blocks, dtype=jnp.int32)
    span = own[:, None] + block_ids[None, :] * counts[:, None] // blocks + shifts
    span = jnp.clip(span, 0, seq_rows - lengths)
    before = own - jnp.concatenate([counts[:1], counts[:-1]])
    slot_rows = low + slot_of * capacity
    base_before = jnp.where(
        members == 0, low - own, jnp.concatenate([slot_rows[:1], slot_rows[:-1]]) - before
    )
    base_own = slot_rows - own
    base_after = (
        jnp.where(
            members == g - 1,
            low + g * capacity,
            jnp.concatenate([slot_rows[1:], slot_rows[-1:]]),
        )
        - after
    )
    is_before = span < own[:, None]
    is_own = span < after[:, None]
    first_base = jnp.where(
        is_before, base_before[:, None], jnp.where(is_own, base_own[:, None], base_after[:, None])
    )
    second_base = jnp.where(is_before, base_own[:, None], base_after[:, None])
    cut = jnp.where(
        is_before, own[:, None] - span, jnp.where(is_own, after[:, None] - span, block_size)
    )
    cut = jnp.minimum(cut, block_size)
    last_start = low + g * capacity + high
    first_start = jnp.clip(span + first_base, 0, last_start)
    second_start = jnp.clip(span + second_base, 0, last_start)
    info = jnp.stack(
        [first_start, second_start, cut, lengths]
    ).reshape(-1).astype(jnp.int32)

    flat = scales.reshape(-1)
    previous = jnp.maximum(q * g - 1, 0)
    pieces = [
        lax.dynamic_slice(
            flat, (previous * capacity + jnp.take(teacher_counts, previous) - low,), (low,)
        )
    ]
    for e in range(g):
        pieces.append(
            lax.dynamic_slice(flat, ((q * g + partner(p, e, g)[0]) * capacity,), (capacity,))
        )
    pieces.append(
        lax.dynamic_slice(flat, (jnp.minimum(q * g + g, n - 1) * capacity,), (high,))
    )
    row_scales = jnp.concatenate(pieces)
    tiles = -(-(last_start + 2 * block_size) // block_size)
    row_scales = jnp.pad(row_scales, (0, tiles * block_size - row_scales.shape[0]))
    row_scales = row_scales.reshape(tiles, 1, block_size)
    weights = weights.reshape(g * blocks, block_size, block_size)
    mixed = mix(g, blocks, info, row_scales, mapped, below, above, weights)
    row_grad, gain_grad = finish(
        g, n, tp, mixed.reshape(g, rows_here, nl * width), student_rows, student_gain[None, :], width
    )
    return (row_grad, gain_grad.reshape(-1))


def solution(mesh):
    placed = (
        P("seq", "tp"),
        P("tp"),
        P(),
        P("tp", "seq"),
        P("seq", "tp"),
        P("tp"),
        P("seq"),
        P("seq"),
        P("seq", None),
    )
    return jax.shard_map(
        shards, mesh=mesh, in_specs=placed, out_specs=(P("seq", "tp"), P("tp")), check_vma=False
    )
```
